32 devices in a mesh: dp: 8 (over z, x), blk: 4 (over y, core).
Axes of the slice: x: 2, y: 2, z: 4, core: 2. Of those that a mesh axis runs over, the one named last changes fastest.
Arguments:
- tokens: bfloat16 [8, 1024, 1152], P('dp', 'blk'), may hold values from -6 to 6
- condition: bfloat16 [8, 7, 1152], P('dp'), may hold values from -6 to 6
- segment_ids: int32 [8, 1024], P('dp'), may hold values from 0 to 6, as said below
- qkv_weight: bfloat16 [1152, 3456], P('dp'), may hold values from -0.1875 to 0.1875
- query_bias: bfloat16 [1152], replicated, may hold values from -1.75 to 1.75
- value_bias: bfloat16 [1152], replicated, may hold values from -1.75 to 1.75
- output_weight: bfloat16 [1152, 1152], P('dp'), may hold values from -1.75 to 1.75
- output_bias: bfloat16 [1152], replicated, may hold values from -1.75 to 1.75
- up_weight: bfloat16 [1152, 4608], P('dp'), may hold values from -0.1875 to 0.1875
- up_bias: bfloat16 [4608], replicated, may hold values from -1.75 to 1.75
- down_weight: bfloat16 [4608, 1152], P('dp'), may hold values from -0.1875 to 0.1875
- down_bias: bfloat16 [1152], replicated, may hold values from -1.75 to 1.75
- adaln_weight: bfloat16 [1152, 6912], P('dp'), may hold values from -0.1875 to 0.1875
- adaln_bias: bfloat16 [6912], replicated, may hold values from -1.75 to 1.75
- cotangent: bfloat16 [8, 1024, 1152], P('dp', 'blk'), may hold values from -6 to 6
Outputs:
- output: bfloat16 [8, 1024, 1152], P('dp', 'blk')
- grad_tokens: bfloat16 [8, 1024, 1152], P('dp', 'blk')
- grad_condition: float32 [8, 7, 1152], P('dp')
- grad_qkv_weight: float32 [1152, 3456], P('dp')
- grad_query_bias: float32 [1152], replicated
- grad_value_bias: float32 [1152], replicated
- grad_output_weight: float32 [1152, 1152], P('dp')
- grad_output_bias: float32 [1152], replicated
- grad_up_weight: float32 [1152, 4608], P('dp')
- grad_up_bias: float32 [4608], replicated
- grad_down_weight: float32 [4608, 1152], P('dp')
- grad_down_bias: float32 [1152], replicated
- grad_adaln_weight: float32 [1152, 6912], P('dp')
- grad_adaln_bias: float32 [6912], replicated
The draws below stay inside these ranges and needn't reach their ends.
Inputs may be any that keep to these rules, and one draw needn't show every extreme that they name: `segment_ids`: Non-decreasing along each sequence, every crop 0 to 6 present; in every sequence one crop begins within the first 256 tokens and ends within the last 256.
All inputs are finite; a program needn't handle non-finite values.
Results may differ from the reference program's by a relative error of at most 0.018.
Values may be sent and summed in bfloat16 or wider, within the bound.
A program may use at most 320 MiB of HBM per device.

```python
import jax
import jax.numpy as jnp
from jax import lax

D = 1152
HEADS = 16
FF = 4608
LEN = 1024
CUTS = 2
NSEQ = 8
STRIP = 256
CROPS = 7
MODW = 6912


def draw_segment_ids(key, part):
    key = jax.random.fold_in(key, 11)
    first_key, second_key, third_key = jax.random.split(key, 3)
    starts = jax.random.randint(first_key, (NSEQ, 1), STRIP // 2, STRIP)
    finish = jax.random.randint(second_key, (NSEQ, 1), LEN - STRIP + 1, LEN - STRIP // 2 + 1)
    places = jnp.arange(LEN, dtype=jnp.int32)[None, :]
    ranking = jax.random.randint(third_key, (NSEQ, LEN), 0, 4096) * LEN + places
    ceiling = 4096 * LEN
    left_rank = jnp.where((places >= 1) & (places < starts), ranking, ceiling + places)
    right_rank = jnp.where(places > finish, ranking, ceiling + places)
    left_cuts = lax.top_k(-left_rank, CUTS)[1].astype(jnp.int32)
    right_cuts = lax.top_k(-right_rank, CUTS)[1].astype(jnp.int32)
    cut_places = jnp.concatenate([starts, finish, left_cuts, right_cuts], axis=1)
    boundary = jnp.sum((places[:, :, None] == cut_places[:, None, :]).astype(jnp.int32), axis=2)
    return jnp.cumsum(boundary, axis=1).astype(jnp.int32)


def block_scale(rng, shape, shards, least, top_value):
    factor_of, own = 1.0, jax.random.fold_in(rng, 6)
    for axis_at, parts in shards:
        heights = jnp.exp(jax.random.uniform(jax.random.fold_in(own, axis_at), (parts,), jnp.float32, least / len(shards), top_value / len(shards)))
        factor_of = factor_of * jnp.repeat(heights, shape[axis_at] // parts).reshape([-1 if axis == axis_at else 1 for axis in range(len(shape))])
    return factor_of


def scatter_about(own_key, shape, scale, reach, pieces=(), kind=jnp.bfloat16):
    array = scale * jax.random.normal(own_key, shape, jnp.float32)
    if pieces:
        array = array * block_scale(own_key, shape, pieces, -0.22, 0.18)
    return jnp.clip(array, -reach, reach).astype(kind)


def setup_inputs(seed: int = 0) -> dict:
    keys = jax.random.split(jax.random.key(seed), 16)
    return {
        "tokens": scatter_about(keys[0], (NSEQ, LEN, D), 1.0, 6.0, ((0, 8), (1, 4))),
        "condition": scatter_about(keys[1], (NSEQ, CROPS, D), 1.0, 6.0, ((0, 8),)),
        "segment_ids": draw_segment_ids(jax.random.fold_in(keys[15], 71), 0),
        "qkv_weight": scatter_about(keys[3], (D, 3 * D), D ** -0.5, 0.1875, ((0, 8),)),
        "query_bias": scatter_about(keys[4], (D,), 0.3, 1.75),
        "value_bias": scatter_about(keys[5], (D,), 0.3, 1.75),
        "output_weight": scatter_about(keys[6], (D, D), (max(D // 96, 4)) ** -0.5, 1.75, ((0, 8),)),
        "output_bias": scatter_about(keys[7], (D,), 0.3, 1.75),
        "up_weight": scatter_about(keys[8], (D, FF), D ** -0.5, 0.1875, ((0, 8),)),
        "up_bias": scatter_about(keys[9], (FF,), 0.3, 1.75),
        "down_weight": scatter_about(keys[10], (FF, D), (FF // 4) ** -0.5, 0.1875, ((0, 8),)),
        "down_bias": scatter_about(keys[11], (D,), 0.3, 1.75),
        "adaln_weight": scatter_about(keys[12], (D, MODW), D ** -0.5, 0.1875, ((0, 8),)),
        "adaln_bias": scatter_about(keys[13], (MODW,), 0.3, 1.75),
        "cotangent": scatter_about(keys[14], (NSEQ, LEN, D), 1.0, 6.0, ((0, 8), (1, 4))),
    }


@jax.custom_vjp
def low(v):
    return lax.optimization_barrier(v.astype(jnp.bfloat16)).astype(jnp.float32)

@jax.custom_vjp
def low_back(v):
    return v

def low_keep(v):
    return (low(v), None)

def low_pass(kept, grad):
    return (grad,)

def back_keep(v):
    return (v, None)

def back_low(kept, grad):
    return (low(grad),)
low.defvjp(low_keep, low_pass)
low_back.defvjp(back_keep, back_low)
highest = lax.Precision.HIGHEST

def modulate(rows, shift, scale):
    centre = rows - lax.optimization_barrier(jnp.mean(rows, axis=-1, keepdims=True))
    normed = centre * lax.rsqrt(lax.optimization_barrier(jnp.mean(centre * centre, axis=-1, keepdims=True)) + 1e-06)
    return normed * (1.0 + scale) + shift

def gelu_tanh(values):
    return jax.nn.gelu(values, approximate=True)

def rounded_both(values):
    return low(low_back(values))

def sequence_layer(weights, tokens, modulation, labels):
    qkv_weight, query_bias, value_bias, output_weight, output_bias, up_weight, up_bias, down_weight, down_bias = weights
    width = tokens.shape[-1]
    head_dim = width // HEADS
    per_token = jnp.take(modulation, labels, axis=0)
    shift_a, scale_a, gate_a, shift_m, scale_m, gate_m = jnp.split(per_token, 6, axis=-1)
    normed_a = low(modulate(tokens, shift_a, scale_a))
    packed_bias = jnp.concatenate([query_bias, jnp.zeros((width,), jnp.float32), value_bias])
    packed = rounded_both(jnp.dot(normed_a, qkv_weight, precision=highest) + packed_bias)
    queries, key_rows, value_rows = jnp.split(packed, 3, axis=-1)
    queries = queries.reshape(-1, HEADS, head_dim)
    key_rows = key_rows.reshape(-1, HEADS, head_dim)
    value_rows = value_rows.reshape(-1, HEADS, head_dim)
    scores = jnp.einsum('qhd,khd->hqk', queries, key_rows, precision=highest) * head_dim ** (-0.5)
    scores = low_back(scores)
    allowed = labels[:, None] == labels[None, :]
    scores = jnp.where(allowed[None], scores, -1e+30)
    row_top = lax.optimization_barrier(jnp.max(scores, axis=-1, keepdims=True))
    raised = jnp.exp(scores - row_top)
    soft_weights = low(raised / lax.optimization_barrier(jnp.sum(raised, axis=-1, keepdims=True)))
    attended = jnp.einsum('hqk,khd->qhd', soft_weights, value_rows, precision=highest).reshape(-1, width)
    attended = rounded_both(attended)
    branch_a = low_back(jnp.dot(attended, output_weight, precision=highest) + output_bias)
    middle = tokens + gate_a * branch_a
    normed_m = low(modulate(middle, shift_m, scale_m))
    hidden = low_back(jnp.dot(normed_m, up_weight, precision=highest) + up_bias)
    active = low(gelu_tanh(hidden))
    branch_m = low_back(jnp.dot(active, down_weight, precision=highest) + down_bias)
    return middle + gate_m * branch_m

def layer(tokens, condition, qkv_weight, query_bias, value_bias, output_weight, output_bias, up_weight, up_bias, down_weight, down_bias, adaln_weight, adaln_bias, labels):
    cond_act = low(jax.nn.silu(condition))
    modulation = jnp.einsum('scd,de->sce', cond_act, adaln_weight, precision=highest) + adaln_bias
    weights = (qkv_weight, query_bias, value_bias, output_weight, output_bias, up_weight, up_bias, down_weight, down_bias)

    def single(member):
        return sequence_layer(weights, member[0], member[1], member[2])
    return lax.map(jax.checkpoint(single), (tokens, modulation, labels))

def reference(tokens, condition, segment_ids, qkv_weight, query_bias, value_bias, output_weight, output_bias, up_weight, up_bias, down_weight, down_bias, adaln_weight, adaln_bias, cotangent):
    floats = tuple((member.astype(jnp.float32) for member in (tokens, condition, qkv_weight, query_bias, value_bias, output_weight, output_bias, up_weight, up_bias, down_weight, down_bias, adaln_weight, adaln_bias)))

    def forward(*inputs):
        return layer(*inputs, segment_ids)
    result, backward = jax.vjp(forward, *floats)
    grads = backward(cotangent.astype(jnp.float32))
    return (result.astype(jnp.bfloat16), grads[0].astype(jnp.bfloat16), grads[1], grads[2], grads[3], grads[4], grads[5], grads[6], grads[7], grads[8], grads[9], grads[10], grads[11], grads[12])
```

```python
import functools
import math

import jax
import jax.numpy as jnp
from jax import lax
from jax.experimental import pallas as pl
from jax.experimental.pallas import tpu as pltpu
from jax.sharding import PartitionSpec as P

HEADS = 16
BLKS = 4
BF = jnp.bfloat16
F32 = jnp.float32
MESH = pl.DeviceIdType.MESH
EPS = 1e-06


def up_to(value, multiple):
    return -(-value // multiple) * multiple


def nn(a, b):
    return lax.dot_general(a, b, (((1,), (0,)), ((), ())), preferred_element_type=F32)


def nt(a, b):
    return lax.dot_general(a, b, (((1,), (1,)), ((), ())), preferred_element_type=F32)


def tn(a, b):
    return lax.dot_general(a, b, (((0,), (0,)), ((), ())), preferred_element_type=F32)


def exact(a, b):
    return lax.dot_general(
        a, b, (((1,), (0,)), ((), ())), precision=lax.Precision.HIGHEST, preferred_element_type=F32
    )


def unit_rows(rows):
    centre = rows - jnp.mean(rows, axis=-1, keepdims=True)
    inverse = lax.rsqrt(jnp.mean(centre * centre, axis=-1, keepdims=True) + EPS)
    return centre * inverse, inverse


def norm_back(grad, normed, inverse):
    mean_grad = jnp.mean(grad, axis=-1, keepdims=True)
    mean_both = jnp.mean(grad * normed, axis=-1, keepdims=True)
    return inverse * (grad - mean_grad - normed * mean_both)


def layer_kernel(dims, *refs):
    T, D, n, sub, R, Q, HD, hpd, F, Fr, MODW = dims
    L, C3, WH, nz = BLKS * T, 3 * Q, D // 2, n // 2
    CP = up_to(C3, 128)
    MQ = up_to(-(-MODW // BLKS), 256)
    WE, WL = up_to(5 * D, 1024), up_to(2 * D + 4 * up_to(Q, 128), 1024)
    QE, QL = WE // 4, WL // 4
    QP = up_to(Q, 128)
    factor = HD ** (-0.5)
    (
        x_in, cot_in, lab_col, lab_row, lab_own, cond_in, adaln_b, qkv_b, out_b, up_b, down_b,
        ad_h, wq_h, wo_h, wu_h, wd_h,
        out_o, gtok_o, dcond_o, ball_e, ball_l, gd_o, gu_o, gq_o, gw_o, na_h,
        wq, wo, wu, wd, ad, cond_rx, pm_tx, pm_rx, mod4, modf,
        na, dbm, act, gp, q3, lse, att_tx, att_rx, datt_tx, mid, bra,
        ps, rs_a, rs_b, gd, gu, gw, gd_x, gu_x, gq_x, gw_x, gd_z, gu_z, gq_z, gw_z,
        fin_d, fin_u, fin_q, fin_w, dk_acc, dv_acc, sb_e, sb_l, btx_e, btx_l, brx_e, brx_l, dc_tx,
        loc, g_s, g_r, c_s, c_r, p_s, p_r, m_s, m_r, ag_s, ag_r, a_s, a_r, r_s, r_r,
        x_s, x_r, z_s, z_r, f_s, f_r, b1_s, b1_r, b2_s, b2_r, b3_s, b3_r, d_s, d_r, w_s, w_r,
    ) = refs

    dp = lax.axis_index("dp")
    b = lax.axis_index("blk")
    g, member = dp // sub, dp % sub
    zi, xi = g // 2, g % 2
    core = b % 2
    b1, b2, b3 = b + 1 - 2 * core, (b + 2) % 4, 3 - b

    def rel(k):
        return ((b // 2 + k // 2) % 2) * 2 + (b % 2 + k % 2) % 2

    def at_dp(group):
        return (group * sub + member, b)

    def at_blk(index):
        return (dp, index)

    gx = g + 1 - 2 * xi

    def gz(k):
        return ((zi + k) % nz) * 2 + xi

    def remote(src, dst, ssem, rsem, where):
        return pltpu.make_async_remote_copy(
            src_ref=src, dst_ref=dst, send_sem=ssem, recv_sem=rsem, device_id=where, device_id_type=MESH
        )

    def strip(i):
        return pl.ds(pl.multiple_of(T * i, T), T)

    def rows_of(i, size):
        return pl.ds(pl.multiple_of(size * i, size), size)

    barrier = pltpu.get_barrier_semaphore()
    for k in range(1, n):
        pl.semaphore_signal(barrier, inc=1, device_id=at_dp((g + k) % n), device_id_type=MESH)
    for other in (b1, b2, b3):
        pl.semaphore_signal(barrier, inc=1, device_id=at_blk(other), device_id_type=MESH)
    pl.semaphore_wait(barrier, n - 1 + 3)

    cond_rx[g] = cond_in[g]
    cond_cp = [
        remote(cond_in.at[(g + k) % n], cond_rx.at[g], c_s.at[k], c_r.at[k], at_dp((g + k) % n))
        for k in range(1, n)
    ]
    for cp in cond_cp:
        cp.start()

    def place_q(i):
        return wq.at[rows_of(i, R), :]

    def place_o(i):
        return wo.at[core, rows_of(i, R), :]

    def place_u(i):
        return wu.at[rows_of(i, R), :]

    def place_d(i):
        return wd.at[rows_of(i, Fr), :]

    class Gather:
        def __init__(self, slot, src, place):
            self.src, self.place = src, place
            self.local = pltpu.make_async_copy(src, place(g), loc.at[slot])
            self.x0 = remote(src, place(g), g_s.at[slot, 0], g_r.at[slot, 0], at_dp(gx))
            self.z = {}
            self.x = {}
            for k in range(1, nz):
                self.z[k] = remote(src, place(g), g_s.at[slot, k], g_r.at[slot, k], at_dp(gz(k)))
                came = ((zi - k + nz) % nz) * 2 + xi
                self.x[k] = remote(
                    place(came), place(came), g_s.at[slot, nz + k], g_r.at[slot, nz + k], at_dp(gx)
                )

        def start(self):
            self.local.start()
            for k in list(range(2, nz)) + [1]:
                self.z[k].start()
            self.x0.start()

        def forward(self):
            for k in range(1, nz):
                self.z[k].wait_recv()
                self.x[k].start()

        def arrive(self):
            self.local.wait()
            self.x0.wait_recv()
            for k in range(1, nz):
                self.x[k].wait_recv()

        def done(self):
            self.x0.wait_send()
            for k in range(1, nz):
                self.z[k].wait_send()
                self.x[k].wait_send()

    take_q = Gather(0, wq_h, place_q)
    take_o = Gather(1, wo_h.at[core], place_o)
    take_u = Gather(2, wu_h, place_u)
    take_d = Gather(3, wd_h, place_d)
    start = pl.multiple_of(jnp.minimum(MQ * b, MODW - MQ), 128)
    ad_cp = pltpu.make_async_copy(ad_h.at[:, pl.ds(start, MQ)], ad, loc.at[4])
    ad_cp.start()
    take_q.start()

    for cp in cond_cp:
        cp.wait_recv()
    ad_cp.wait()
    cond_all = cond_rx[...].reshape(n * 8, R).astype(BF)
    partial = nn(cond_all, ad[...]).reshape(n, 8, MQ)
    halves = jnp.concatenate([partial[:, :, : MQ // 2], partial[:, :, MQ // 2 :]], axis=1)
    pm_tx[...] = halves.astype(BF)
    pm_rx[g] = pm_tx[g]
    part_cp = [
        remote(pm_tx.at[(g + k) % n], pm_rx.at[g], p_s.at[k], p_r.at[k], at_dp((g + k) % n))
        for k in range(1, n)
    ]
    for cp in part_cp:
        cp.start()
    rows_in = x_in[...].astype(F32)
    normed, _ = unit_rows(rows_in)
    for cp in part_cp:
        cp.wait_recv()
    total = jnp.sum(pm_rx[...].astype(F32), axis=0)
    own_mod = jnp.concatenate([total[:8], total[8:]], axis=1) + adaln_b[:, pl.ds(start, MQ)]
    mod4[b] = own_mod
    mod_cp = [
        remote(mod4.at[b], mod4.at[b], m_s.at[k], m_r.at[k], at_blk(rel(k))) for k in range(1, 4)
    ]
    for cp in mod_cp:
        cp.start()
    for cp in mod_cp:
        cp.wait_recv()
    for j in range(BLKS):
        first = min(MQ * j, MODW - MQ)
        skip = MQ * j - first
        modf[:, MQ * j : min(MQ * (j + 1), MODW)] = mod4[j][:, skip:]
    chooser = (lab_own[...] == lax.broadcasted_iota(jnp.int32, (T, 8), 1)).astype(F32)

    def per_token(piece):
        return exact(chooser, modf[:, D * piece : D * (piece + 1)])

    class Spread:
        def __init__(self, slot, buffer):
            def copy(index, src, where):
                return remote(
                    buffer.at[strip(src), :], buffer.at[strip(src), :], ag_s.at[slot, index], ag_r.at[slot, index],
                    at_blk(where),
                )

            self.near = copy(0, b, b1)
            self.far = copy(1, b, b2)
            self.onward = copy(2, b2, b1)

        def start(self):
            self.far.start()
            self.near.start()

        def forward(self):
            self.far.wait_recv()
            self.onward.start()

        def done(self):
            self.near.wait_send()
            self.far.wait_send()
            self.onward.wait_send()

    na[strip(b), :] = (normed * (1.0 + per_token(1)) + per_token(0)).astype(BF)
    spread_a = Spread(0, na)
    spread_a.start()
    upstream = cot_in[...].astype(F32)
    d_branch_m = (per_token(5) * upstream).astype(BF)
    dbm[strip(b), :] = d_branch_m
    sb_e[...] = jnp.zeros_like(sb_e)
    sb_l[...] = jnp.zeros_like(sb_l)
    sb_e[1:2, 4 * D : 5 * D] = jnp.sum(d_branch_m.astype(F32), axis=0, keepdims=True)
    take_o.start()
    take_u.start()
    take_q.forward()
    take_q.arrive()

    def project(k):
        i = rel(k)
        packed = nn(na[strip(i), :], wq[...]) + qkv_b[...]
        for s in range(3 * hpd):
            q3[s, strip(i), :] = packed[:, HD * s : HD * (s + 1)].astype(BF)

    def project_loop(lo, hi):
        def body(k, carry):
            project(k)
            return carry

        lax.fori_loop(lo, hi, body, 0)

    project_loop(0, 1)
    spread_a.near.wait_recv()
    project_loop(1, 2)
    spread_a.forward()
    project_loop(2, 3)
    spread_a.onward.wait_recv()
    project_loop(3, 4)
    keep_na = pltpu.make_async_copy(na, na_h, loc.at[5])
    keep_na.start()
    spread_d = Spread(1, dbm)
    spread_d.start()
    take_d.start()

    def attend(i):
        mask = lab_col[strip(i), :] == lab_row[...]
        pieces, logs = [], []
        for h in range(hpd):
            scores = nt(q3[h, strip(i), :], q3[hpd + h]) * factor
            scores = jnp.where(mask, scores, -1e30)
            top = jnp.max(scores, axis=-1, keepdims=True)
            raised = jnp.exp(scores - top)
            sums = jnp.sum(raised, axis=-1, keepdims=True)
            pieces.append(nn(raised.astype(BF), q3[2 * hpd + h]) / sums)
            logs.append(top + jnp.log(sums))
        att_tx[i] = jnp.concatenate(pieces, axis=1).astype(BF)
        lse[strip(i), :] = jnp.concatenate(logs, axis=1)

    att_cp = {
        k: remote(att_tx.at[rel(k)], att_rx.at[b], a_s.at[0, k], a_r.at[0, k], at_blk(rel(k)))
        for k in range(1, 4)
    }
    for turn, k in enumerate((2, 3, 1, 0)):
        attend(rel(k))
        if turn == 0:
            keep_na.wait()
            spread_a.done()
        if k:
            att_cp[k].start()
        if turn == 0:
            take_o.forward()
        if turn == 1:
            take_o.arrive()
            share_o = remote(wo.at[core], wo.at[core], g_s.at[1, 2 * nz], g_r.at[1, 2 * nz], at_blk(b1))
            share_o.start()
        if turn == 2:
            spread_d.forward()
    att_rx[b] = att_tx[b]
    take_u.forward()
    for k in range(1, 4):
        att_cp[k].wait_recv()
    share_o.wait_recv()
    attf = jnp.concatenate([att_rx[j] for j in range(BLKS)], axis=1)
    branch_a = jnp.concatenate([nn(attf, wo[0]), nn(attf, wo[1])], axis=1) + out_b[...]
    bra[...] = branch_a
    middle = rows_in_again(x_in) + per_token(2) * branch_a
    mid[...] = middle
    normed, _ = unit_rows(middle)
    na[strip(b), :] = (normed * (1.0 + per_token(4)) + per_token(3)).astype(BF)
    spread_m = Spread(2, na)
    spread_m.start()
    take_u.arrive()

    c0, c1 = math.sqrt(2.0 / math.pi), 0.044715

    def feed(k):
        i = rel(k)
        hidden = nn(na[strip(i), :], wu[...]) + up_b[...]
        square = hidden * hidden
        bent = jnp.tanh(c0 * (hidden + c1 * hidden * square))
        half = 0.5 * (1.0 + bent)
        act[strip(i), :] = (hidden * half).astype(BF)
        slope = half + 0.5 * hidden * (1.0 - bent * bent) * (c0 * (1.0 + (3.0 * c1) * square))
        gp[strip(i), :] = slope.astype(BF)

    def feed_down(k):
        i = rel(k)
        ps[i] = nn(act[strip(i), :], wd[...]).astype(BF)

    def loop(lo, hi, step):
        def body(k, carry):
            step(k)
            return carry

        lax.fori_loop(lo, hi, body, 0)

    class Reduce:
        def __init__(self, slot, rx):
            self.rx = rx
            self.near = remote(ps.at[b1], rx.at[0], r_s.at[slot, 0], r_r.at[slot, 0], at_blk(b1))
            self.pair = remote(ps.at[b3], rx.at[1], r_s.at[slot, 1], r_r.at[slot, 1], at_blk(b1))
            self.far = remote(ps.at[b2], rx.at[2], r_s.at[slot, 2], r_r.at[slot, 2], at_blk(b2))

        def cross(self):
            self.pair.wait_recv()
            ps[b2] = (ps[b2].astype(F32) + self.rx[1].astype(F32)).astype(BF)
            self.far.start()

        def result(self):
            self.near.wait_recv()
            self.far.wait_recv()
            total = ps[b].astype(F32) + self.rx[0].astype(F32) + self.rx[2].astype(F32)
            self.near.wait_send()
            self.pair.wait_send()
            self.far.wait_send()
            return total

    loop(0, 1, feed)
    spread_m.near.wait_recv()
    loop(1, 2, feed)
    take_d.forward()
    spread_m.forward()
    loop(2, 3, feed)
    spread_m.onward.wait_recv()
    loop(3, 4, feed)
    take_d.arrive()
    reduce_f = Reduce(0, rs_a)
    loop(3, 4, feed_down)
    reduce_f.pair.start()
    loop(2, 3, feed_down)
    reduce_f.cross()
    loop(1, 2, feed_down)
    reduce_f.near.start()
    loop(0, 1, feed_down)

    spread_d.near.wait_recv()
    spread_d.onward.wait_recv()

    class Scatter:
        def __init__(self, slot, grad, rows, xrx, zrx, fin, dest):
            cols = self.cols = fin.shape[1]
            self.slot, self.grad, self.rows, self.xrx, self.zrx, self.fin, self.dest = slot, grad, rows, xrx, zrx, fin, dest
            self.x, self.z = {}, {}
            for k in range(nz):
                z_at = (zi + k) % nz
                self.x[k] = remote(
                    grad.at[rows_of(2 * z_at + 1 - xi, rows), pl.ds(0, cols)], xrx.at[z_at],
                    x_s.at[slot, k], x_r.at[slot, k], at_dp(gx),
                )
                if k:
                    self.z[k] = remote(
                        xrx.at[z_at], zrx.at[nz - k - 1], z_s.at[slot, k], z_r.at[slot, nz - k], at_dp(gz(k))
                    )
            self.local = pltpu.make_async_copy(fin, dest.at[b], loc.at[6 + slot])
            self.near = remote(fin, dest.at[b], f_s.at[slot, 0], f_r.at[slot, 0], at_blk(b1))
            self.far = remote(fin, dest.at[b], f_s.at[slot, 1], f_r.at[slot, 1], at_blk(b2))
            self.onward = remote(dest.at[b2], dest.at[b2], f_s.at[slot, 2], f_r.at[slot, 2], at_blk(b1))

        def start(self):
            for k in list(range(1, nz)) + [0]:
                self.x[k].start()

        def cross(self):
            for k in range(1, nz):
                z_at = (zi + k) % nz
                self.x[k].wait_recv()
                own = self.grad[rows_of(2 * z_at + xi, self.rows), 0 : self.cols].astype(F32)
                self.xrx[z_at] = (own + self.xrx[z_at].astype(F32)).astype(BF)
                self.z[k].start()

        def total(self):
            self.x[0].wait_recv()
            own = self.grad[rows_of(g, self.rows), 0 : self.cols].astype(F32) + self.xrx[zi].astype(F32)
            for k in range(1, nz):
                remote(
                    self.xrx.at[0], self.zrx.at[k - 1], z_s.at[0, 0], z_r.at[self.slot, k], at_dp(gx)
                ).wait_recv()
                own = own + self.zrx[k - 1].astype(F32)
            self.fin[...] = own.astype(BF)
            self.far.start()
            self.near.start()
            self.local.start()

        def forward(self):
            self.far.wait_recv()
            self.onward.start()

        def done(self):
            self.near.wait_recv()
            self.onward.wait_recv()
            self.local.wait()
            self.near.wait_send()
            self.far.wait_send()
            self.onward.wait_send()
            for k in range(nz):
                self.x[k].wait_send()
                if k:
                    self.z[k].wait_send()


    give_d = Scatter(0, gd, Fr, gd_x, gd_z, fin_d, gd_o)
    give_u = Scatter(1, gu, R, gu_x, gu_z, fin_u, gu_o)
    give_q = Scatter(2, wu, R, gq_x, gq_z, fin_q, gq_o)

    def hidden_back(k):
        i = rel(k)
        d_active = nt(dbm[strip(i), :], wd[...])
        gp[strip(i), :] = (gp[strip(i), :].astype(F32) * d_active).astype(BF)

    def tiles(size):
        return 384 if size % 384 == 0 else size

    def weight_grad(dest, left, right, size):
        step = tiles(size)

        def body(j, carry):
            at = pl.ds(pl.multiple_of(step * j, step), step)
            dest[at, :] = tn(left[:, at], right[...]).astype(BF)
            return carry

        lax.fori_loop(0, size // step, body, 0)

    loop(0, 4, hidden_back)
    weight_grad(gd, act, dbm, F)
    give_d.start()
    weight_grad(gu, na, gp, D)
    give_u.start()
    at_e7 = pl.ds(pl.multiple_of(F * b, 128), F)

    one_hot = (lax.broadcasted_iota(jnp.int32, (8, T), 0) == lab_row[:, strip(b)]).astype(F32)

    def per_crop(values):
        return exact(one_hot, values)

    branch_m = reduce_f.result() + down_b[...]
    out_o[...] = (mid[...] + per_token(5) * branch_m).astype(BF)
    sb_e[:, 3 * D : 4 * D] = per_crop(cot_in[...].astype(F32) * branch_m)

    def up_back(k):
        i = rel(k)
        ps[i] = nt(gp[strip(i), :], wu[...]).astype(BF)

    spread_d.done()
    reduce_m = Reduce(1, rs_b)
    loop(3, 4, up_back)
    reduce_m.pair.start()
    loop(2, 3, up_back)
    reduce_m.cross()
    loop(1, 2, up_back)
    reduce_m.near.start()
    loop(0, 1, up_back)
    na_back = pltpu.make_async_copy(na_h, na, loc.at[5])
    spread_m.done()
    na_back.start()
    up_sums = jnp.sum(gp[...].astype(F32), axis=0, keepdims=True)
    give_d.cross()
    d_normed = reduce_m.result()
    normed, inverse = unit_rows(mid[...])
    d_middle = cot_in[...].astype(F32) + norm_back(d_normed * (1.0 + per_token(4)), normed, inverse)
    mid[...] = d_middle
    d_branch_a = (per_token(2) * d_middle).astype(BF)

    d_att = (nt(d_branch_a[:, :WH], wo[0]) + nt(d_branch_a[:, WH:], wo[1])).astype(BF)
    for j in range(BLKS):
        datt_tx[j] = d_att[:, Q * j : Q * (j + 1)]
    datt_cp = {
        k: remote(datt_tx.at[rel(k)], att_rx.at[b], a_s.at[1, k], a_r.at[1, k], at_blk(rel(k)))
        for k in range(1, 4)
    }
    for k in (2, 3, 1):
        datt_cp[k].start()
    dbm[strip(b), :] = d_branch_a
    spread_w = Spread(3, dbm)
    spread_w.start()
    att_rx[b] = datt_tx[b]
    sb_e[:, 0:D] = per_crop(d_middle * bra[...])
    sb_e[:, D : 2 * D] = per_crop(d_normed)
    sb_e[:, 2 * D : 3 * D] = per_crop(d_normed * normed)
    sb_e[7:8, at_e7] = up_sums
    sb_e[0:1, 4 * D : 5 * D] = jnp.sum(d_branch_a.astype(F32), axis=0, keepdims=True)

    class Bundle:
        def __init__(self, slot, sums, tx, rx, ball, quarter):
            self.sums, self.tx, self.rx, self.ball, self.quarter = sums, tx, rx, ball, quarter
            self.one = [
                remote(tx.at[rel(k)], rx.at[b], b1_s.at[slot, k], b1_r.at[slot, k], at_blk(rel(k)))
                for k in range(1, 4)
            ]
            self.two = [
                remote(ball.at[b, g], ball.at[b, g], b2_s.at[slot, k], b2_r.at[slot, k], at_dp((g + k) % n))
                for k in range(1, n)
            ]
            self.three = [
                remote(ball.at[b], ball.at[b], b3_s.at[slot, k], b3_r.at[slot, k], at_blk(rel(k)))
                for k in range(1, 4)
            ]

        def start(self):
            half = self.quarter // 2
            for j in range(BLKS):
                first = self.sums[:, 2 * half * j : 2 * half * j + half]
                second = self.sums[:, 2 * half * j + half : 2 * half * (j + 1)]
                self.tx[j] = jnp.concatenate([first, second], axis=0).astype(BF)
            self.rx[b] = self.tx[b]
            for cp in self.one:
                cp.start()

        def groups(self):
            for cp in self.one:
                cp.wait_recv()
            self.ball[b, g] = jnp.sum(self.rx[...].astype(F32), axis=0).astype(BF)
            for cp in self.two:
                cp.start()

        def share(self):
            for cp in self.two:
                cp.wait_recv()
            for cp in self.three:
                cp.start()

        def arrive(self):
            for cp in self.three:
                cp.wait_recv()

        def done(self):
            for cp in self.one + self.two + self.three:
                cp.wait_send()

    bundle_e = Bundle(0, sb_e, btx_e, brx_e, ball_e, QE)
    bundle_l = Bundle(1, sb_l, btx_l, brx_l, ball_l, QL)
    bundle_e.start()
    for k in range(1, 4):
        datt_cp[k].wait_recv()

    def head_back(h):
        dk_acc[...] = jnp.zeros_like(dk_acc)
        dv_acc[...] = jnp.zeros_like(dv_acc)

        def body(i, carry):
            at = strip(i)
            query, keys, values = q3[h, at, :], q3[hpd + h], q3[2 * hpd + h]
            mask = lab_col[at, :] == lab_row[...]
            scores = jnp.where(mask, nt(query, keys) * factor, -1e30)
            probs = jnp.exp(scores - lse[at, h : h + 1])
            d_out = att_rx[i, :, HD * h : HD * (h + 1)]
            kept = att_tx[i, :, HD * h : HD * (h + 1)]
            delta = jnp.sum(d_out.astype(F32) * kept.astype(F32), axis=-1, keepdims=True)
            dv_acc[...] += tn(probs.astype(BF), d_out)
            d_scores = (probs * (nt(d_out, values) - delta)).astype(BF)
            dk_acc[...] += tn(d_scores, query)
            q3[h, at, :] = (nn(d_scores, keys) * factor).astype(BF)
            return carry

        lax.fori_loop(0, BLKS, body, 0)
        q3[hpd + h] = (dk_acc[...] * factor).astype(BF)
        q3[2 * hpd + h] = dv_acc[...].astype(BF)

    class OutScatter:
        def __init__(self):
            self.x = remote(gw.at[rows_of(1 - xi, R), :], gw_x, w_s.at[0], w_r.at[0], at_dp(gx))
            at = jnp.maximum((zi - b + nz) % nz, 1) - 1
            self.z = remote(gw_x, gw_z.at[at], w_s.at[1], w_r.at[1 + at], at_dp(2 * b + xi))
            self.local = pltpu.make_async_copy(fin_w, gw_o, loc.at[9])
            self.out = [
                remote(fin_w, gw_o, w_s.at[1 + k], w_r.at[nz + 1], at_blk(rel(k))) for k in range(1, 4)
            ]

        def start(self):
            self.x.start()

        def cross(self):
            self.x.wait_recv()
            total = gw[rows_of(xi, R), :].astype(F32) + gw_x[...].astype(F32)
            gw_x[...] = total.astype(BF)

            @pl.when(zi != b)
            def _():
                self.z.start()

        def total(self):
            @pl.when(zi == b)
            def _():
                own = gw_x[...].astype(F32)
                for k in range(1, nz):
                    remote(gw_x, gw_z.at[k - 1], w_s.at[0], w_r.at[k], at_dp(gx)).wait_recv()
                    own = own + gw_z[k - 1].astype(F32)
                fin_w[...] = own.astype(BF)
                for cp in self.out:
                    cp.start()
                self.local.start()

        def done(self):
            self.x.wait_send()

            @pl.when(zi != b)
            def _():
                self.z.wait_send()
                self.out[0].wait_recv()

            @pl.when(zi == b)
            def _():
                for cp in self.out:
                    cp.wait_send()
                self.local.wait()

    take_d.done()
    pieces_cp = [
        pltpu.make_async_copy(ad_h.at[:, pl.ds(D * p, D)], wd.at[pl.ds(R * p, R), pl.ds(0, D)], loc.at[10 + p])
        for p in range(6)
    ]
    for cp in pieces_cp:
        cp.start()
    give_w = OutScatter()
    head_back(0)
    give_d.total()
    give_u.cross()
    bundle_e.groups()
    spread_w.forward()
    head_back(1)
    bundle_e.share()
    spread_w.near.wait_recv()
    spread_w.onward.wait_recv()
    att_all = att_tx[...].reshape(L, Q)
    gw[...] = tn(att_all, dbm[...]).astype(BF)
    give_w.start()
    give_d.forward()
    head_back(2)
    give_u.total()
    give_w.cross()
    head_back(3)
    give_u.forward()
    give_w.total()

    def back_rows(i):
        return jnp.concatenate([q3[s, strip(i), :] for s in range(3 * hpd)], axis=1)

    def qkv_back(k):
        i = rel(k)
        d_packed = back_rows(i)
        act[strip(i), 0:C3] = d_packed
        ps[i] = nt(d_packed, wq[...]).astype(BF)

    reduce_a = Reduce(2, rs_a)
    loop(3, 4, qkv_back)
    reduce_a.pair.start()
    loop(2, 3, qkv_back)
    reduce_a.cross()
    loop(1, 2, qkv_back)
    reduce_a.near.start()
    loop(0, 1, qkv_back)
    na_back.wait()
    take_u.done()
    step = tiles(D)

    def grad_body(j, carry):
        at = pl.ds(pl.multiple_of(step * j, step), step)
        wu[at, 0:C3] = tn(na[:, at], act[:, 0:C3]).astype(BF)
        return carry

    lax.fori_loop(0, D // step, grad_body, 0)
    give_q.start()
    bias_sums = jnp.sum(act[:, 0:C3].astype(F32), axis=0, keepdims=True)
    pad = jnp.zeros((1, QP - Q), F32)
    at_l = pl.ds(pl.multiple_of(2 * D + QP * b, 128), QP)
    sb_l[0:1, at_l] = jnp.concatenate([bias_sums[:, :Q], pad], axis=1)
    sb_l[1:2, at_l] = jnp.concatenate([bias_sums[:, 2 * Q :], pad], axis=1)
    d_normed = reduce_a.result()
    normed, inverse = unit_rows(rows_in_again(x_in))
    sb_l[:, 0:D] = per_crop(d_normed)
    sb_l[:, D : 2 * D] = per_crop(d_normed * normed)
    bundle_l.start()
    gtok_o[...] = (mid[...] + norm_back(d_normed * (1.0 + per_token(1)), normed, inverse)).astype(BF)
    bundle_l.groups()
    give_q.cross()
    bundle_e.arrive()
    for cp in pieces_cp:
        cp.wait()

    def crop_part(ball, j, columns, half, first, width):
        both = ball[j].astype(F32)
        rows = both[:, 0:8, :] if half == 0 else both[:, 8:16, :]
        rows = rows.reshape(n * 8, columns).astype(BF)
        total, at = 0.0, first
        while at < first + width:
            p = at // D
            end = min(first + width, D * (p + 1))
            total = total + nt(rows[:, at - first : end - first], wd[R * p : R * (p + 1), at - D * p : end - D * p])
            at = end
        return total

    d_cond = jnp.zeros((n * 8, R), F32)
    for j in range(BLKS):
        for half in range(2):
            first = QE * j + half * (QE // 2)
            width = min(QE // 2, 4 * D - first)
            if width > 0:
                d_cond = d_cond + crop_part(ball_e, j, QE // 2, half, 2 * D + first, width)
    bundle_l.share()
    bundle_l.arrive()
    for j in range(BLKS):
        for half in range(2):
            first = QL * j + half * (QL // 2)
            width = min(QL // 2, 2 * D - first)
            if width > 0:
                d_cond = d_cond + crop_part(ball_l, j, QL // 2, half, first, width)
    dc_tx[...] = d_cond.reshape(n, 8, R)
    dcond_o[g] = dc_tx[g]
    dcond_cp = [
        remote(dc_tx.at[(g + k) % n], dcond_o.at[g], d_s.at[k], d_r.at[k], at_dp((g + k) % n))
        for k in range(1, n)
    ]
    for cp in dcond_cp:
        cp.start()
    give_q.total()
    give_q.forward()
    for cp in dcond_cp:
        cp.wait_recv()

    give_q.done()
    give_d.done()
    give_u.done()
    give_w.done()
    bundle_e.done()
    bundle_l.done()
    for cp in cond_cp + part_cp + mod_cp + dcond_cp:
        cp.wait_send()
    for k in range(1, 4):
        att_cp[k].wait_send()
        datt_cp[k].wait_send()
    spread_w.done()
    share_o.wait_send()
    for take in (take_q, take_o):
        take.done()


def rows_in_again(x_in):
    return x_in[...].astype(F32)


def run_layer(dims, inputs, n_out):
    T, D, n, sub, R, Q, HD, hpd, F, Fr, MODW = dims
    L, C3, WH, nz = BLKS * T, 3 * Q, D // 2, n // 2
    CP = up_to(C3, 128)
    MQ = up_to(-(-MODW // BLKS), 256)
    WE, WL = up_to(5 * D, 1024), up_to(2 * D + 4 * up_to(Q, 128), 1024)
    vm = pl.BlockSpec(memory_space=pltpu.VMEM)
    hbm = pl.BlockSpec(memory_space=pl.ANY)
    out_shape = (
        jax.ShapeDtypeStruct((T, D), BF),
        jax.ShapeDtypeStruct((T, D), BF),
        jax.ShapeDtypeStruct((n, 8, R), F32),
        jax.ShapeDtypeStruct((BLKS, n, 16, WE // 8), BF),
        jax.ShapeDtypeStruct((BLKS, n, 16, WL // 8), BF),
        jax.ShapeDtypeStruct((BLKS, Fr, D), BF),
        jax.ShapeDtypeStruct((BLKS, R, F), BF),
        jax.ShapeDtypeStruct((BLKS, R, CP), BF),
        jax.ShapeDtypeStruct((R, D), BF),
        jax.ShapeDtypeStruct((L, D), BF),
    )
    dma = pltpu.SemaphoreType.DMA
    scratch = [
        pltpu.VMEM((D, C3), BF),
        pltpu.VMEM((2, D, WH), BF),
        pltpu.VMEM((D, F), BF),
        pltpu.VMEM((F, D), BF),
        pltpu.VMEM((R, MQ), BF),
        pltpu.VMEM((n, 8, R), F32),
        pltpu.VMEM((n, 16, MQ // 2), BF),
        pltpu.VMEM((n, 16, MQ // 2), BF),
        pltpu.VMEM((BLKS, 8, MQ), F32),
        pltpu.VMEM((8, MODW), F32),
        pltpu.VMEM((L, D), BF),
        pltpu.VMEM((L, D), BF),
        pltpu.VMEM((L, F), BF),
        pltpu.VMEM((L, F), BF),
        pltpu.VMEM((3 * hpd, L, HD), BF),
        pltpu.VMEM((L, hpd), F32),
        pltpu.VMEM((BLKS, T, Q), BF),
        pltpu.VMEM((BLKS, T, Q), BF),
        pltpu.VMEM((BLKS, T, Q), BF),
        pltpu.VMEM((T, D), F32),
        pltpu.VMEM((T, D), F32),
        pltpu.VMEM((BLKS, T, D), BF),
        pltpu.VMEM((3, T, D), BF),
        pltpu.VMEM((3, T, D), BF),
        pltpu.VMEM((F, D), BF),
        pltpu.VMEM((D, F), BF),
        pltpu.VMEM((Q, D), BF),
        pltpu.VMEM((nz, Fr, D), BF),
        pltpu.VMEM((nz, R, F), BF),
        pltpu.VMEM((nz, R, CP), BF),
        pltpu.VMEM((R, D), BF),
        pltpu.VMEM((nz - 1, Fr, D), BF),
        pltpu.VMEM((nz - 1, R, F), BF),
        pltpu.VMEM((nz - 1, R, CP), BF),
        pltpu.VMEM((nz - 1, R, D), BF),
        pltpu.VMEM((Fr, D), BF),
        pltpu.VMEM((R, F), BF),
        pltpu.VMEM((R, CP), BF),
        pltpu.VMEM((R, D), BF),
        pltpu.VMEM((L, HD), F32),
        pltpu.VMEM((L, HD), F32),
        pltpu.VMEM((8, WE), F32),
        pltpu.VMEM((8, WL), F32),
        pltpu.VMEM((BLKS, 16, WE // 8), BF),
        pltpu.VMEM((BLKS, 16, WL // 8), BF),
        pltpu.VMEM((BLKS, 16, WE // 8), BF),
        pltpu.VMEM((BLKS, 16, WL // 8), BF),
        pltpu.VMEM((n, 8, R), F32),
        dma((16,)),
        dma((4, 2 * nz + 1)), dma((4, 2 * nz + 1)),
        dma((n,)), dma((n,)), dma((n,)), dma((n,)),
        dma((4,)), dma((4,)),
        dma((4, 3)), dma((4, 3)),
        dma((2, 4)), dma((2, 4)),
        dma((3, 3)), dma((3, 3)),
        dma((3, nz)), dma((3, nz)), dma((3, nz)), dma((3, nz)),
        dma((3, 3)), dma((3, 3)),
        dma((2, 4)), dma((2, 4)), dma((2, n)), dma((2, n)), dma((2, 4)), dma((2, 4)),
        dma((n,)), dma((n,)),
        dma((nz + 2,)), dma((nz + 2,)),
    ]
    in_specs = [vm] * 11 + [hbm] * 5
    out_specs = [vm] * 5 + [hbm] * 5
    return pl.pallas_call(
        functools.partial(layer_kernel, dims),
        out_shape=out_shape,
        in_specs=in_specs,
        out_specs=out_specs,
        scratch_shapes=scratch,
        compiler_params=pltpu.CompilerParams(
            collective_id=0, has_side_effects=True, vmem_limit_bytes=63 << 20
        ),
        name="layer",
    )(*inputs)


def per_device(sub, tokens, condition, segment_ids, qkv_weight, query_bias, value_bias, output_weight, output_bias,
               up_weight, up_bias, down_weight, down_bias, adaln_weight, adaln_bias, cotangent):
    T, D = tokens.shape[1:]
    blks, size = lax.axis_size("blk"), lax.axis_size("dp")
    assert blks == BLKS and tokens.shape[0] == 1
    n = size // sub
    HD = D // HEADS
    hpd = HEADS // blks
    Q = D // blks
    FF = up_weight.shape[1]
    MODW = adaln_weight.shape[1]
    F = FF // blks
    R, Fr = D // n, F // n
    b = lax.axis_index("blk")
    dp = lax.axis_index("dp")

    def members(step):
        return [(i, i - i % sub + (i + step) % sub) for i in range(size)]

    def collect(w):
        if sub == 1:
            return w
        full = jnp.zeros((sub,) + w.shape, w.dtype)
        for step in range(sub):
            moved = lax.ppermute(w, "dp", members(step)) if step else w
            full = lax.dynamic_update_index_in_dim(full, moved, (dp - step) % sub, 0)
        return full.reshape((-1,) + w.shape[1:])

    def settle(grad):
        if sub == 1:
            return grad
        parts = grad.reshape((sub, -1) + grad.shape[1:])
        total = 0.0
        for step in range(sub):
            part = lax.dynamic_index_in_dim(parts, (dp + step) % sub, 0, keepdims=False)
            total = total + (lax.ppermute(part, "dp", members(step)) if step else part)
        return total

    def over_members(vector):
        if sub == 1:
            return vector
        total = vector
        for step in range(1, sub):
            total = total + lax.ppermute(vector, "dp", members(step))
        return total

    def pick(w, groups, width):
        return lax.dynamic_index_in_dim(w.reshape(w.shape[0], groups, blks, width), b, 2, keepdims=False).reshape(
            w.shape[0], groups * width
        )

    qkv_own = pick(collect(qkv_weight), 3, Q)
    out_own = collect(output_weight).reshape(R, 2, D // 2).transpose(1, 0, 2)
    up_own = pick(collect(up_weight), n, Fr)
    down_own = lax.dynamic_slice_in_dim(collect(down_weight), b * Fr, Fr, 0)
    adaln_own = collect(adaln_weight)
    qkv_bias = jnp.concatenate([query_bias, jnp.zeros_like(query_bias), value_bias]).astype(F32)[None]
    crops = condition.shape[1]
    cond = condition[0].astype(F32)
    cond_act, silu_back = jax.vjp(jax.nn.silu, cond)
    cond_low = cond_act.astype(BF).astype(F32)
    cond_rows = jnp.pad(cond_low, ((0, 8 - crops), (0, 0))).reshape(8, n, R).transpose(1, 0, 2)
    own_labels = lax.dynamic_slice_in_dim(segment_ids, b * T, T, 1)
    inputs = (
        tokens[0], cotangent[0], segment_ids.reshape(-1, 1), segment_ids, own_labels.reshape(T, 1), cond_rows,
        adaln_bias.astype(F32)[None], pick(qkv_bias, 3, Q), output_bias.astype(F32)[None],
        pick(up_bias.astype(F32)[None], n, Fr), down_bias.astype(F32)[None],
        adaln_own, qkv_own, out_own, up_own, down_own,
    )
    dims = (T, D, n, sub, R, Q, HD, hpd, F, Fr, MODW)
    out, gtok, dcond, ball_e, ball_l, gd, gu, gq, gw, _ = run_layer(dims, inputs, 10)

    def crops_of(ball):
        half = ball.shape[-1]
        return ball.reshape(blks, n, 2, 8, half).transpose(1, 3, 0, 2, 4).reshape(n, 8, blks * 2 * half).astype(F32)

    early, late = crops_of(ball_e), crops_of(ball_l)
    QP = up_to(Q, 128)
    d_mod = jnp.concatenate([late[:, :crops, : 2 * D], early[:, :crops, : 4 * D]], axis=-1)
    cond_all = cond_rows_all(cond_low, n, sub, members, dp, R, crops)
    grad_adaln = jnp.einsum("scd,sce->de", cond_all.astype(BF), d_mod.astype(BF), preferred_element_type=F32)
    early_sum, late_sum = over_members(jnp.sum(early, axis=0)), over_members(jnp.sum(late, axis=0))
    grad_adaln_bias = over_members(jnp.sum(d_mod, axis=(0, 1)))
    grad_output_bias = early_sum[0, 4 * D : 5 * D]
    grad_down_bias = early_sum[1, 4 * D : 5 * D]
    grad_up_bias = early_sum[7, :FF].reshape(blks, n, Fr).transpose(1, 0, 2).reshape(FF)
    slots = late_sum[:2, 2 * D : 2 * D + 4 * QP].reshape(2, blks, QP)[:, :, :Q].reshape(2, D)
    d_cond_act = dcond.transpose(1, 0, 2).reshape(8, D)[:crops]
    grad_condition = silu_back(d_cond_act)[0][None]
    grad_qkv = gq[:, :, : 3 * Q].astype(F32).reshape(blks, R, 3, Q).transpose(1, 2, 0, 3).reshape(R, 3 * D)
    grad_up = gu.astype(F32).reshape(blks, R, n, Fr).transpose(1, 2, 0, 3).reshape(R, FF)
    grad_down = gd.astype(F32).reshape(blks * Fr, D)
    return (
        out[None], gtok[None], grad_condition, settle(grad_qkv), slots[0], slots[1], settle(gw.astype(F32)),
        grad_output_bias, settle(grad_up), grad_up_bias, settle(grad_down), grad_down_bias, settle(grad_adaln),
        grad_adaln_bias,
    )


def cond_rows_all(cond_low, n, sub, members, dp, R, crops):
    size = n * sub
    g = dp // sub
    blocks = cond_low.reshape(crops, n, R).transpose(1, 0, 2)
    full = jnp.zeros((n, crops, R), F32)
    for step in range(n):
        part = lax.dynamic_index_in_dim(blocks, (g + step) % n, 0, keepdims=False)
        perm = [(i, ((i // sub + step) % n) * sub + i % sub) for i in range(size)]
        moved = lax.ppermute(part, "dp", perm) if step else part
        full = lax.dynamic_update_index_in_dim(full, moved, (g - step) % n, 0)
    return full


def solution(mesh):
    rows, strips = P("dp", None), P("dp", "blk", None)
    in_specs = (
        strips, P("dp", None, None), rows, rows, P(), P(), rows, P(), rows, P(), rows, P(), rows, P(), strips,
    )
    out_specs = (
        strips, strips, P("dp", None, None), rows, P(), P(), rows, P(), rows, P(), rows, P(), rows, P(),
    )

    def whole(*args):
        size = mesh.shape["dp"]
        rows_each = args[3].shape[0] // size
        sub = 1
        while (rows_each * sub) % 16:
            sub *= 2
        body = functools.partial(per_device, sub)
        return jax.shard_map(body, mesh=mesh, in_specs=in_specs, out_specs=out_specs, check_vma=False)(*args)

    return whole
```

```python
import functools
import math

import jax
import jax.numpy as jnp
from jax import lax
from jax.experimental import pallas as pl
from jax.experimental.pallas import tpu as pltpu
from jax.sharding import PartitionSpec as P

HEADS = 16
BLKS = 4
BF = jnp.bfloat16
F32 = jnp.float32
MESH = pl.DeviceIdType.MESH
EPS = 1e-06


def up_to(value, multiple):
    return -(-value // multiple) * multiple


def nn(a, b):
    return lax.dot_general(a, b, (((1,), (0,)), ((), ())), preferred_element_type=F32)


def nt(a, b):
    return lax.dot_general(a, b, (((1,), (1,)), ((), ())), preferred_element_type=F32)


def tn(a, b):
    return lax.dot_general(a, b, (((0,), (0,)), ((), ())), preferred_element_type=F32)


def row_sums(values):
    return nn(jnp.ones((8, values.shape[0]), BF), values)[0:1]


def unit_rows(rows):
    centre = rows - jnp.mean(rows, axis=-1, keepdims=True)
    inverse = lax.rsqrt(jnp.mean(centre * centre, axis=-1, keepdims=True) + EPS)
    return centre * inverse, inverse


def norm_back(grad, normed, inverse):
    mean_grad = jnp.mean(grad, axis=-1, keepdims=True)
    mean_both = jnp.mean(grad * normed, axis=-1, keepdims=True)
    return inverse * (grad - mean_grad - normed * mean_both)


def layer_kernel(dims, *refs):
    T, D, n, sub, R, Q, HD, hpd, F, Fr, MODW = dims
    L, C3, WH, nz = BLKS * T, 3 * Q, D // 2, n // 2
    CP = up_to(C3, 128)
    MQ = up_to(-(-MODW // BLKS), 256)
    WE, WL = up_to(5 * D, 1024), up_to(2 * D + 4 * up_to(Q, 128), 1024)
    QE, QL = WE // 4, WL // 4
    QP = up_to(Q, 128)
    factor = HD ** (-0.5)
    (
        x_in, cot_in, lab_row, cond_in, query_b, value_b, out_bias, down_bias, up_bias, ad_bias,
        ad_h, wq_h, wo_h, wu_h, wd_h,
        out_o, gtok_o, cond_rx, dcond_o, ball_e, ball_l, gd_o, gu_o, gq_o, gw_o, na_h,
        wq, wo, wu, wd, ad, qkv_b, up_b, ad_b, cond_tx, pm_tx, pm_rx, mod4, mod3,
        na, dbm, act, gp, q3, lse, att_tx, att_rx, datt_tx, mid, dmid, bra,
        ps, rs_a, rs_b, gd, gu, gw, gd_x, gu_x, gq_x, gw_x, gw_z,
        fin_w, dk_acc, dv_acc, sb_e, sb_l, btx_e, btx_l, brx_e, brx_l, dc_tx,
        loc, g_s, g_r, o_s, o_r, c_s, c_r, p_s, p_r, m_s, m_r, ag_s, ag_r, a_s, a_r, r_s, r_r,
        x_s, x_r, f_s, f_r, b1_s, b1_r, b2_s, b2_r, b3_s, b3_r, d_s, d_r, w_s, w_r,
    ) = refs

    dp = lax.axis_index("dp")
    b = lax.axis_index("blk")
    g, member = dp // sub, dp % sub
    zi, xi = g // 2, g % 2
    core = b % 2
    b1, b2, b3 = b + 1 - 2 * core, (b + 2) % 4, 3 - b

    def rel(k):
        return ((b // 2 + k // 2) % 2) * 2 + (b % 2 + k % 2) % 2

    def at_dp(group):
        return (group * sub + member, b)

    def at_blk(index):
        return (dp, index)

    gx = g + 1 - 2 * xi

    place = zi + xi * (n - 1 - 2 * zi)
    first_rows = up_to(R // 2, 16)

    def group_at(position):
        position = (position + 2 * n) % n
        back = position // nz
        return 2 * (position + back * (n - 1 - 2 * position)) + back

    def remote(src, dst, ssem, rsem, where):
        return pltpu.make_async_remote_copy(
            src_ref=src, dst_ref=dst, send_sem=ssem, recv_sem=rsem, device_id=where, device_id_type=MESH
        )

    def strip(i):
        return pl.ds(pl.multiple_of(T * i, T), T)

    def rows_of(i, size):
        return pl.ds(pl.multiple_of(size * i, size), size)

    FF = BLKS * F
    stage_cp = [
        pltpu.make_async_copy(src.at[:, pl.ds(D * p, D)], gd.at[pl.ds(R * to, R), :], loc.at[10 + to])
        for to, (src, p) in enumerate(
            [(wq_h, 0), (wq_h, 1), (wq_h, 2), (wo_h, 0), (wu_h, 0), (wu_h, 1), (wu_h, 2), (wu_h, 3)]
        )
    ]
    for cp in stage_cp:
        cp.start()
    own_d = pltpu.make_async_copy(wd_h.at[rows_of(b, Fr), :], wd.at[rows_of(g, Fr), :], loc.at[3])
    own_d.start()

    def flat(ref):
        return ref[...].astype(F32).reshape(1, -1)

    ad_b[...] = flat(ad_bias)

    barrier = pltpu.get_barrier_semaphore()
    for k in range(1, n):
        pl.semaphore_signal(barrier, inc=1, device_id=at_dp((g + k) % n), device_id_type=MESH)
    for other in (b1, b2, b3):
        pl.semaphore_signal(barrier, inc=1, device_id=at_blk(other), device_id_type=MESH)
    pl.semaphore_wait(barrier, n - 1 + 3)

    cond = cond_in[...].astype(F32)
    cond = (cond / (1.0 + jnp.exp(-cond))).astype(BF).astype(F32)
    cond = jnp.concatenate([cond, jnp.zeros((8 - cond.shape[0], D), F32)], axis=0)
    for gg in range(n):
        cond_tx[gg] = cond[:, R * gg : R * (gg + 1)]
    cond_rx[g] = cond_tx[g]
    cond_cp = [
        remote(cond_tx.at[(g + k) % n], cond_rx.at[g], c_s.at[k], c_r.at[k], at_dp((g + k) % n))
        for k in range(1, n)
    ]
    for cp in cond_cp:
        cp.start()

    def piece(size, i, half):
        first = first_rows if half else 0
        return pl.ds(pl.multiple_of(size * i + first, 16), size - first_rows if half else first_rows)

    class Gather:
        def __init__(self, slot, ref):
            self.copies = {}
            for way in range(2):
                sign = 1 - 2 * way
                for half in range(2):
                    for step in range(nz if half == way else nz - 1):
                        at = ref.at[piece(R, group_at(place - sign * step), half), :]
                        flow = 2 * way + half
                        self.copies[way, half, step] = remote(
                            at, at, g_s.at[slot, flow, step], g_r.at[slot, flow, step], at_dp(group_at(place + sign))
                        )

        def start(self):
            for half in range(2):
                for way in range(2):
                    self.copies[way, half, 0].start()

        def hop(self, step):
            for half in range(2):
                for way in range(2):
                    self.copies[way, half, step - 1].wait_recv()
                    if (way, half, step) in self.copies:
                        self.copies[way, half, step].start()

        def arrive(self):
            for way in range(2):
                self.copies[way, way, nz - 1].wait_recv()

        def done(self):
            for copy in self.copies.values():
                copy.wait_send()

    take_q, take_o = Gather(0, wq), Gather(1, wo.at[core])
    take_u, take_d = Gather(2, wu), Gather(3, wd)
    for cp in stage_cp[:3]:
        cp.wait()
    for j in range(BLKS):

        @pl.when(b == j)
        def _():
            own = [gd[R * p : R * (p + 1), Q * j : Q * (j + 1)] for p in range(3)]
            wq[rows_of(g, R), :] = jnp.concatenate(own, axis=1)

    take_q.start()
    start = pl.multiple_of(jnp.minimum(MQ * b, MODW - MQ), 128)
    ad_cp = pltpu.make_async_copy(ad_h.at[:, pl.ds(start, MQ)], ad, loc.at[4])
    ad_cp.start()

    for cp in cond_cp:
        cp.wait_recv()
    ad_cp.wait()
    cond_all = cond_rx[...].reshape(n * 8, R).astype(BF)
    partial = nn(cond_all, ad[...]).reshape(n, 8, MQ)
    halves = jnp.concatenate([partial[:, :, : MQ // 2], partial[:, :, MQ // 2 :]], axis=1)
    pm_tx[...] = halves.astype(BF)
    pm_rx[g] = pm_tx[g]
    part_cp = [
        remote(pm_tx.at[(g + k) % n], pm_rx.at[g], p_s.at[k], p_r.at[k], at_dp((g + k) % n))
        for k in range(1, n)
    ]
    for cp in part_cp:
        cp.start()
    for cp in stage_cp[3:]:
        cp.wait()
    for j in range(BLKS):

        @pl.when(b == j)
        def _():
            own = [
                gd[R * (4 + (p // D)) : R * (5 + (p // D)), p % D : p % D + Fr]
                for p in range(Fr * j, FF, BLKS * Fr)
            ]
            wu[rows_of(g, R), :] = jnp.concatenate(own, axis=1)
            at = slice(Q * j, Q * (j + 1))
            parts = [flat(query_b)[:, at], jnp.zeros((1, Q), F32), flat(value_b)[:, at]]
            qkv_b[...] = jnp.concatenate(parts, axis=1)
            every = flat(up_bias)
            own = [every[:, p : p + Fr] for p in range(Fr * j, FF, BLKS * Fr)]
            up_b[...] = jnp.concatenate(own, axis=1)

    for j in range(2):

        @pl.when(core == j)
        def _():
            wo[j, rows_of(g, R), :] = gd[3 * R : 4 * R, WH * j : WH * (j + 1)]

    one_hot = lab_row[...] == lax.broadcasted_iota(jnp.int32, (8, L), 0)
    column = lax.broadcasted_iota(jnp.int32, (8, 128), 0).astype(BF)
    labels = tn(one_hot.astype(BF), column)
    lse[:, hpd : hpd + 1] = labels[:, 0:1]
    row_labels = lab_row[...].astype(F32)
    take_q.hop(1)
    for cp in part_cp:
        cp.wait_recv()
    total = jnp.sum(pm_rx[...].astype(F32), axis=0)
    own_mod = jnp.concatenate([total[:8], total[8:]], axis=1) + ad_b[:, pl.ds(start, MQ)]
    mod4[b] = own_mod
    mod_cp = [
        remote(mod4.at[b], mod4.at[b], m_s.at[k], m_r.at[k], at_blk(rel(k))) for k in range(1, 4)
    ]
    for cp in mod_cp:
        cp.start()
    for cp in mod_cp:
        cp.wait_recv()
    for j in range(BLKS):
        first = min(MQ * j, MODW - MQ)
        skip = MQ * j - first
        value = mod4[j][:, skip:]
        high = value.astype(BF).astype(F32)
        middle = (value - high).astype(BF).astype(F32)
        parts = jnp.concatenate([high, middle, value - high - middle], axis=0)
        mod3[:, MQ * j : min(MQ * (j + 1), MODW)] = parts.astype(BF)
    CH = T // 2

    def by_chunk(step):
        def body(c, carry):
            step(pl.ds(pl.multiple_of(CH * c, CH), CH), pl.ds(pl.multiple_of(T * b + CH * c, CH), CH))
            return carry

        lax.fori_loop(0, T // CH, body, 0)

    def crop_of(rows, width):
        crops = jnp.bitwise_and(lax.broadcasted_iota(jnp.int32, (CH, width), 1), 7).astype(F32)
        return (lse[rows, hpd : hpd + 1] == crops).astype(BF)

    def per_token(chooser, piece):
        return nn(chooser, mod3[:, D * piece : D * (piece + 1)])

    def per_crop(chooser, values):
        high = values.astype(BF)
        return tn(chooser, high) + tn(chooser, (values - high.astype(F32)).astype(BF))

    class Spread:
        def __init__(self, slot, buffer):
            def copy(index, src, where):
                return remote(
                    buffer.at[strip(src), :], buffer.at[strip(src), :], ag_s.at[slot, index], ag_r.at[slot, index],
                    at_blk(where),
                )

            self.near = copy(0, b, b1)
            self.far = copy(1, b, b2)
            self.onward = copy(2, b2, b1)

        def start(self):
            self.far.start()
            self.near.start()

        def forward(self):
            self.far.wait_recv()
            self.onward.start()

        def done(self):
            self.near.wait_send()
            self.far.wait_send()
            self.onward.wait_send()

    def begin(at, rows):
        normed, _ = unit_rows(x_in[at, :].astype(F32))
        chooser = crop_of(rows, 24)
        na[rows, :] = (normed * (1.0 + per_token(chooser, 1)) + per_token(chooser, 0)).astype(BF)

    by_chunk(begin)
    spread_a = Spread(0, na)
    spread_a.start()

    def begin_back(at, rows):
        dbm[rows, :] = (per_token(crop_of(rows, 24), 5) * cot_in[at, :].astype(F32)).astype(BF)

    by_chunk(begin_back)
    sb_e[...] = jnp.zeros_like(sb_e)
    sb_l[...] = jnp.zeros_like(sb_l)
    sb_e[1:2, 4 * D : 5 * D] = row_sums(dbm[strip(b), :])
    take_q.hop(2)
    take_q.hop(3)
    take_o.start()
    take_q.arrive()

    def project(k):
        i = rel(k)
        packed = nn(na[strip(i), :], wq[...]) + qkv_b[...]
        for s in range(3 * hpd):
            q3[s, strip(i), :] = packed[:, HD * s : HD * (s + 1)].astype(BF)

    def project_loop(lo, hi):
        def body(k, carry):
            project(k)
            return carry

        lax.fori_loop(lo, hi, body, 0)

    project_loop(0, 1)
    spread_a.near.wait_recv()
    project_loop(1, 2)
    spread_a.forward()
    project_loop(2, 3)
    take_o.hop(1)
    spread_a.onward.wait_recv()
    project_loop(3, 4)
    keep_na = pltpu.make_async_copy(na, na_h, loc.at[5])
    keep_na.start()
    spread_d = Spread(1, dbm)
    spread_d.start()
    own_d.wait()

    def attend(i):
        mask = lse[strip(i), hpd : hpd + 1] == row_labels
        pieces, logs = [], []
        for h in range(hpd):
            scores = nt(q3[h, strip(i), :], q3[hpd + h]) * factor
            scores = jnp.where(mask, scores, -1e30)
            top = jnp.max(scores, axis=-1, keepdims=True)
            raised = jnp.exp(scores - top)
            sums = jnp.sum(raised, axis=-1, keepdims=True)
            pieces.append(nn(raised.astype(BF), q3[2 * hpd + h]) / sums)
            logs.append(top + jnp.log(sums))
        att_tx[i] = jnp.concatenate(pieces, axis=1).astype(BF)
        lse[strip(i), 0:hpd] = jnp.concatenate(logs, axis=1)

    att_cp = {
        k: remote(att_tx.at[rel(k)], att_rx.at[b], a_s.at[0, k], a_r.at[0, k], at_blk(rel(k)))
        for k in range(1, 4)
    }
    for turn, k in enumerate((2, 3, 1, 0)):
        attend(rel(k))
        if turn == 0:
            keep_na.wait()
            spread_a.done()
        if k:
            att_cp[k].start()
        if turn == 0:
            take_o.hop(2)
        if turn == 1:
            take_o.hop(3)
            take_u.start()
        if turn == 2:
            take_o.arrive()
            share_o = remote(wo.at[core], wo.at[core], o_s.at[0], o_r.at[0], at_blk(b1))
            share_o.start()
        if turn == 3:
            spread_d.forward()
    att_rx[b] = att_tx[b]
    for k in range(1, 4):
        att_cp[k].wait_recv()
    share_o.wait_recv()
    attf = jnp.concatenate([att_rx[j] for j in range(BLKS)], axis=1)
    branch_a = jnp.concatenate([nn(attf, wo[0]), nn(attf, wo[1])], axis=1) + flat(out_bias)
    bra[...] = branch_a

    def between(at, rows):
        chooser = crop_of(rows, 24)
        middle = x_in[at, :].astype(F32) + per_token(chooser, 2) * bra[at, :]
        mid[at, :] = middle
        normed, _ = unit_rows(middle)
        na[rows, :] = (normed * (1.0 + per_token(chooser, 4)) + per_token(chooser, 3)).astype(BF)

    by_chunk(between)
    spread_m = Spread(2, na)
    spread_m.start()

    c0, c1 = math.sqrt(2.0 / math.pi), 0.044715

    def feed(k):
        i = rel(k)
        hidden = nn(na[strip(i), :], wu[...]) + up_b[...]
        square = hidden * hidden
        bent = jnp.tanh(c0 * (hidden + c1 * hidden * square))
        half = 0.5 * (1.0 + bent)
        act[strip(i), :] = (hidden * half).astype(BF)
        slope = half + 0.5 * hidden * (1.0 - bent * bent) * (c0 * (1.0 + (3.0 * c1) * square))
        gp[strip(i), :] = slope.astype(BF)

    def feed_down(k):
        i = rel(k)
        na[strip(i), :] = nn(act[strip(i), :], wd[...]).astype(BF)

    def loop(lo, hi, step):
        def body(k, carry):
            step(k)
            return carry

        lax.fori_loop(lo, hi, body, 0)

    class Reduce:
        def __init__(self, slot, buffer, rx):
            self.buffer, self.rx = buffer, rx

            def copy(index, src, where):
                return remote(
                    buffer.at[strip(src), :], rx.at[index], r_s.at[slot, index], r_r.at[slot, index], at_blk(where)
                )

            self.near, self.pair, self.far = copy(0, b1, b1), copy(1, b3, b1), copy(2, b2, b2)

        def cross(self):
            self.pair.wait_recv()
            total = self.buffer[strip(b2), :].astype(F32) + self.rx[1].astype(F32)
            self.buffer[strip(b2), :] = total.astype(BF)
            self.far.start()

        def arrive(self):
            self.near.wait_recv()
            self.far.wait_recv()
            self.near.wait_send()
            self.pair.wait_send()
            self.far.wait_send()

        def result(self, at, rows):
            total = self.buffer[rows, :].astype(F32) + self.rx[0, at, :].astype(F32)
            return total + self.rx[2, at, :].astype(F32)

    take_u.hop(1)
    spread_m.near.wait_recv()
    take_u.hop(2)
    spread_m.forward()
    take_u.hop(3)
    take_d.start()
    spread_m.onward.wait_recv()
    take_u.arrive()
    loop(0, 4, feed)

    spread_d.near.wait_recv()
    spread_d.onward.wait_recv()

    class Scatter:
        def __init__(self, slot, grad, rx, dest):
            self.grad, self.rx, self.dest, self.cols = grad, rx, dest, rx.shape[3]
            self.copies = {}
            for way in range(2):
                sign = 1 - 2 * way
                for half in range(2):
                    far = nz if half == way else nz - 1
                    for left in range(far):
                        where = piece(R, 0, half)
                        if left == far - 1:
                            owner = group_at(place + sign * far)
                            src = grad.at[piece(R, owner, half), pl.ds(0, self.cols)]
                        else:
                            src = rx.at[way, left + 1, where, :]
                        flow = 2 * way + half
                        self.copies[way, half, left] = remote(
                            src, rx.at[way, left, where, :], x_s.at[slot, flow, left], x_r.at[slot, flow, left],
                            at_dp(group_at(place + sign)),
                        )
            own = rx.at[0, 0]
            self.local = pltpu.make_async_copy(own, dest.at[b], loc.at[6 + slot])
            self.near = remote(own, dest.at[b], f_s.at[slot, 0], f_r.at[slot, 0], at_blk(b1))
            self.far = remote(own, dest.at[b], f_s.at[slot, 1], f_r.at[slot, 1], at_blk(b2))
            self.onward = remote(dest.at[b2], dest.at[b2], f_s.at[slot, 2], f_r.at[slot, 2], at_blk(b1))

        def start(self):
            for way in range(2):
                self.copies[way, way, nz - 1].start()
            for way in range(2):
                self.copies[way, 1 - way, nz - 2].start()

        def pump(self, left):
            for other in (1, 0):
                for way in range(2):
                    half = 1 - way if other else way
                    if left == nz - 1 and other:
                        continue
                    self.copies[way, half, left].wait_recv()
                    owner = group_at(place + (1 - 2 * way) * left)
                    first = first_rows if half else 0
                    last = R if half else first_rows
                    own = self.grad[piece(R, owner, half), 0 : self.cols].astype(F32)
                    total = own + self.rx[way, left, first:last, :].astype(F32)
                    self.rx[way, left, first:last, :] = total.astype(BF)
                    self.copies[way, half, left - 1].start()

        def total(self):
            for way in range(2):
                for half in range(2):
                    self.copies[way, half, 0].wait_recv()
            own = self.grad[rows_of(g, R), 0 : self.cols].astype(F32)
            own = own + self.rx[0, 0].astype(F32) + self.rx[1, 0].astype(F32)
            self.rx[0, 0] = own.astype(BF)
            self.far.start()
            self.near.start()
            self.local.start()

        def forward(self):
            self.far.wait_recv()
            self.onward.start()

        def done(self):
            self.near.wait_recv()
            self.onward.wait_recv()
            self.local.wait()
            self.near.wait_send()
            self.far.wait_send()
            self.onward.wait_send()
            for copy in self.copies.values():
                copy.wait_send()

    give_d = Scatter(0, gd, gd_x, gd_o)
    give_u = Scatter(1, gu, gu_x, gu_o)
    give_q = Scatter(2, wu, gq_x, gq_o)

    def hidden_back(k):
        i = rel(k)
        d_active = nt(dbm[strip(i), :], wd[...])
        gp[strip(i), :] = (gp[strip(i), :].astype(F32) * d_active).astype(BF)

    def tiles(size):
        return 384 if size % 384 == 0 else size

    def weight_grad(dest, left, right, size):
        step = tiles(size)

        def body(j, carry):
            at = pl.ds(pl.multiple_of(step * j, step), step)
            dest[at, :] = tn(left[:, at], right[...]).astype(BF)
            return carry

        lax.fori_loop(0, size // step, body, 0)

    take_d.hop(1)
    weight_grad(gd, act, dbm, F)
    give_d.start()
    take_d.hop(2)
    take_d.hop(3)
    take_d.arrive()
    loop(0, 4, hidden_back)
    give_d.pump(3)
    at_e7 = pl.ds(pl.multiple_of(F * b, 128), F)

    def up_back(k):
        i = rel(k)
        ps[strip(i), :] = nt(gp[strip(i), :], wu[...]).astype(BF)

    spread_d.done()
    reduce_m = Reduce(1, ps, rs_b)
    loop(3, 4, up_back)
    reduce_m.pair.start()
    loop(2, 3, up_back)
    reduce_m.cross()
    loop(1, 2, up_back)
    reduce_m.near.start()
    loop(0, 1, up_back)
    weight_grad(gu, na, gp, D)
    give_u.start()
    give_d.pump(2)
    spread_m.done()
    reduce_f = Reduce(0, na, rs_a)
    loop(3, 4, feed_down)
    reduce_f.pair.start()
    loop(1, 3, feed_down)
    reduce_f.near.start()
    loop(0, 1, feed_down)
    up_sums = row_sums(gp[...])
    give_d.pump(1)
    reduce_m.arrive()

    def middle_back(at, rows):
        d_normed = reduce_m.result(at, rows)
        ps[rows, :] = d_normed.astype(BF)
        normed, inverse = unit_rows(mid[at, :])
        chooser = crop_of(rows, 24)
        d_normed = d_normed * (1.0 + per_token(chooser, 4))
        d_middle = cot_in[at, :].astype(F32) + norm_back(d_normed, normed, inverse)
        dmid[at, :] = d_middle
        dbm[rows, :] = (per_token(chooser, 2) * d_middle).astype(BF)

    by_chunk(middle_back)

    own_rows = dbm[strip(b), :]
    d_att = (nt(own_rows[:, :WH], wo[0]) + nt(own_rows[:, WH:], wo[1])).astype(BF)
    for j in range(BLKS):
        datt_tx[j] = d_att[:, Q * j : Q * (j + 1)]
    datt_cp = {
        k: remote(datt_tx.at[rel(k)], att_rx.at[b], a_s.at[1, k], a_r.at[1, k], at_blk(rel(k)))
        for k in range(1, 4)
    }
    for k in (2, 3, 1):
        datt_cp[k].start()
    spread_w = Spread(3, dbm)
    spread_w.start()
    give_u.pump(3)
    give_d.total()
    reduce_f.cross()
    att_rx[b] = datt_tx[b]

    def middle_sums(at, rows):
        chooser = crop_of(rows, 8)
        normed, _ = unit_rows(mid[at, :])
        d_normed = ps[rows, :].astype(F32)
        sb_e[:, 0:D] += per_crop(chooser, dmid[at, :] * bra[at, :])
        sb_e[:, D : 2 * D] += per_crop(chooser, d_normed)
        sb_e[:, 2 * D : 3 * D] += per_crop(chooser, d_normed * normed)

    by_chunk(middle_sums)
    sb_e[0:1, 4 * D : 5 * D] = row_sums(dbm[strip(b), :])

    class Bundle:
        def __init__(self, slot, sums, tx, rx, ball, quarter):
            self.sums, self.tx, self.rx, self.ball, self.quarter = sums, tx, rx, ball, quarter
            self.one = [
                remote(tx.at[rel(k)], rx.at[b], b1_s.at[slot, k], b1_r.at[slot, k], at_blk(rel(k)))
                for k in range(1, 4)
            ]
            self.two = [
                remote(ball.at[b, g], ball.at[b, g], b2_s.at[slot, k], b2_r.at[slot, k], at_dp((g + k) % n))
                for k in range(1, n)
            ]
            self.three = [
                remote(ball.at[b], ball.at[b], b3_s.at[slot, k], b3_r.at[slot, k], at_blk(rel(k)))
                for k in range(1, 4)
            ]

        def start(self):
            half = self.quarter // 2
            for j in range(BLKS):
                first = self.sums[:, 2 * half * j : 2 * half * j + half]
                second = self.sums[:, 2 * half * j + half : 2 * half * (j + 1)]
                self.tx[j] = jnp.concatenate([first, second], axis=0).astype(BF)
            self.rx[b] = self.tx[b]
            for cp in self.one:
                cp.start()

        def groups(self):
            for cp in self.one:
                cp.wait_recv()
            self.ball[b, g] = jnp.sum(self.rx[...].astype(F32), axis=0).astype(BF)
            for cp in self.two:
                cp.start()

        def share(self):
            for cp in self.two:
                cp.wait_recv()
            for cp in self.three:
                cp.start()

        def arrive(self):
            for cp in self.three:
                cp.wait_recv()

        def done(self):
            for cp in self.one + self.two + self.three:
                cp.wait_send()

    bundle_e = Bundle(0, sb_e, btx_e, brx_e, ball_e, QE)
    bundle_l = Bundle(1, sb_l, btx_l, brx_l, ball_l, QL)
    for k in range(1, 4):
        datt_cp[k].wait_recv()

    def head_back(h):
        dk_acc[...] = jnp.zeros_like(dk_acc)
        dv_acc[...] = jnp.zeros_like(dv_acc)

        def body(i, carry):
            at = strip(i)
            query, keys, values = q3[h, at, :], q3[hpd + h], q3[2 * hpd + h]
            mask = lse[at, hpd : hpd + 1] == row_labels
            scores = jnp.where(mask, nt(query, keys) * factor, -1e30)
            probs = jnp.exp(scores - lse[at, h : h + 1])
            d_out = att_rx[i, :, HD * h : HD * (h + 1)]
            kept = att_tx[i, :, HD * h : HD * (h + 1)]
            delta = jnp.sum(d_out.astype(F32) * kept.astype(F32), axis=-1, keepdims=True)
            dv_acc[...] += tn(probs.astype(BF), d_out)
            d_scores = (probs * (nt(d_out, values) - delta)).astype(BF)
            dk_acc[...] += tn(d_scores, query)
            q3[h, at, :] = (nn(d_scores, keys) * factor).astype(BF)
            return carry

        lax.fori_loop(0, BLKS, body, 0)
        q3[hpd + h] = (dk_acc[...] * factor).astype(BF)
        q3[2 * hpd + h] = dv_acc[...].astype(BF)

    class OutScatter:
        def __init__(self):
            self.x = remote(gw.at[rows_of(1 - xi, R), :], gw_x, w_s.at[0], w_r.at[0], at_dp(gx))
            at = jnp.maximum((zi - b + nz) % nz, 1) - 1
            self.z = remote(gw_x, gw_z.at[at], w_s.at[1], w_r.at[1 + at], at_dp(2 * b + xi))
            self.local = pltpu.make_async_copy(fin_w, gw_o, loc.at[9])
            self.out = [
                remote(fin_w, gw_o, w_s.at[1 + k], w_r.at[nz + 1], at_blk(rel(k))) for k in range(1, 4)
            ]

        def start(self):
            self.x.start()

        def cross(self):
            self.x.wait_recv()
            total = gw[rows_of(xi, R), :].astype(F32) + gw_x[...].astype(F32)
            gw_x[...] = total.astype(BF)

            @pl.when(zi != b)
            def _():
                self.z.start()

        def total(self):
            @pl.when(zi == b)
            def _():
                own = gw_x[...].astype(F32)
                for k in range(1, nz):
                    remote(gw_x, gw_z.at[k - 1], w_s.at[0], w_r.at[k], at_dp(gx)).wait_recv()
                    own = own + gw_z[k - 1].astype(F32)
                fin_w[...] = own.astype(BF)
                for cp in self.out:
                    cp.start()
                self.local.start()

        def done(self):
            self.x.wait_send()

            @pl.when(zi != b)
            def _():
                self.z.wait_send()
                self.out[0].wait_recv()

            @pl.when(zi == b)
            def _():
                for cp in self.out:
                    cp.wait_send()
                self.local.wait()

    take_d.done()
    pieces_cp = [
        pltpu.make_async_copy(ad_h.at[:, pl.ds(D * p, D)], wd.at[pl.ds(R * p, R), pl.ds(0, D)], loc.at[10 + p])
        for p in range(6)
    ]
    for cp in pieces_cp:
        cp.start()
    give_w = OutScatter()
    head_back(0)
    give_u.pump(2)
    spread_w.forward()
    head_back(1)
    give_u.pump(1)
    give_d.forward()
    spread_w.near.wait_recv()
    spread_w.onward.wait_recv()
    att_all = att_tx[...].reshape(L, Q)
    gw[...] = tn(att_all, dbm[...]).astype(BF)
    give_w.start()
    head_back(2)
    reduce_f.arrive()

    def end(at, rows):
        branch_m = reduce_f.result(at, rows) + flat(down_bias)
        out_o[at, :] = (mid[at, :] + per_token(crop_of(rows, 24), 5) * branch_m).astype(BF)
        sb_e[:, 3 * D : 4 * D] += per_crop(crop_of(rows, 8), cot_in[at, :].astype(F32) * branch_m)

    by_chunk(end)
    na_back = pltpu.make_async_copy(na_h, na, loc.at[5])
    na_back.start()
    sb_e[7:8, at_e7] = up_sums
    bundle_e.start()
    give_w.cross()
    head_back(3)
    give_u.total()
    bundle_e.groups()

    def back_rows(i):
        return jnp.concatenate([q3[s, strip(i), :] for s in range(3 * hpd)], axis=1)

    def qkv_back(k):
        i = rel(k)
        d_packed = back_rows(i)
        act[strip(i), 0:C3] = d_packed
        ps[strip(i), :] = nt(d_packed, wq[...]).astype(BF)

    reduce_a = Reduce(2, ps, rs_a)
    loop(3, 4, qkv_back)
    reduce_a.pair.start()
    loop(2, 3, qkv_back)
    reduce_a.cross()
    loop(1, 2, qkv_back)
    reduce_a.near.start()
    loop(0, 1, qkv_back)
    na_back.wait()
    take_u.done()
    step = tiles(D)

    def grad_body(j, carry):
        at = pl.ds(pl.multiple_of(step * j, step), step)
        wu[at, 0:C3] = tn(na[:, at], act[:, 0:C3]).astype(BF)
        return carry

    lax.fori_loop(0, D // step, grad_body, 0)
    give_q.start()
    give_u.forward()
    give_w.total()
    bundle_e.share()
    bias_sums = row_sums(act[:, 0:C3])
    pad = jnp.zeros((1, QP - Q), F32)
    at_l = pl.ds(pl.multiple_of(2 * D + QP * b, 128), QP)
    sb_l[0:1, at_l] = jnp.concatenate([bias_sums[:, :Q], pad], axis=1)
    sb_l[1:2, at_l] = jnp.concatenate([bias_sums[:, 2 * Q :], pad], axis=1)
    reduce_a.arrive()

    def token_sums(at, rows):
        chooser = crop_of(rows, 8)
        normed, _ = unit_rows(x_in[at, :].astype(F32))
        d_normed = reduce_a.result(at, rows)
        sb_l[:, 0:D] += per_crop(chooser, d_normed)
        sb_l[:, D : 2 * D] += per_crop(chooser, d_normed * normed)

    by_chunk(token_sums)
    give_q.pump(3)
    bundle_l.start()

    def token_back(at, rows):
        normed, inverse = unit_rows(x_in[at, :].astype(F32))
        d_normed = reduce_a.result(at, rows) * (1.0 + per_token(crop_of(rows, 24), 1))
        gtok_o[at, :] = (dmid[at, :] + norm_back(d_normed, normed, inverse)).astype(BF)

    by_chunk(token_back)
    bundle_l.groups()
    give_q.pump(2)
    bundle_e.arrive()
    for cp in pieces_cp:
        cp.wait()

    def crop_part(ball, j, columns, half, first, width):
        both = ball[j].astype(F32)
        rows = both[:, 0:8, :] if half == 0 else both[:, 8:16, :]
        rows = rows.reshape(n * 8, columns).astype(BF)
        total, at = 0.0, first
        while at < first + width:
            p = at // D
            end = min(first + width, D * (p + 1))
            total = total + nt(rows[:, at - first : end - first], wd[R * p : R * (p + 1), at - D * p : end - D * p])
            at = end
        return total

    d_cond = jnp.zeros((n * 8, R), F32)
    for j in range(BLKS):
        for half in range(2):
            first = QE * j + half * (QE // 2)
            width = min(QE // 2, 4 * D - first)
            if width > 0:
                d_cond = d_cond + crop_part(ball_e, j, QE // 2, half, 2 * D + first, width)
    bundle_l.share()
    give_q.pump(1)
    bundle_l.arrive()
    for j in range(BLKS):
        for half in range(2):
            first = QL * j + half * (QL // 2)
            width = min(QL // 2, 2 * D - first)
            if width > 0:
                d_cond = d_cond + crop_part(ball_l, j, QL // 2, half, first, width)
    dc_tx[...] = d_cond.reshape(n, 8, R)
    dcond_o[g] = dc_tx[g]
    dcond_cp = [
        remote(dc_tx.at[(g + k) % n], dcond_o.at[g], d_s.at[k], d_r.at[k], at_dp((g + k) % n))
        for k in range(1, n)
    ]
    for cp in dcond_cp:
        cp.start()
    give_q.total()
    give_q.forward()
    for cp in dcond_cp:
        cp.wait_recv()

    give_q.done()
    give_d.done()
    give_u.done()
    give_w.done()
    bundle_e.done()
    bundle_l.done()
    for cp in cond_cp + part_cp + mod_cp + dcond_cp:
        cp.wait_send()
    for k in range(1, 4):
        att_cp[k].wait_send()
        datt_cp[k].wait_send()
    spread_w.done()
    share_o.wait_send()
    for take in (take_q, take_o):
        take.done()


def run_layer(dims, inputs):
    T, D, n, sub, R, Q, HD, hpd, F, Fr, MODW = dims
    L, C3, WH, nz = BLKS * T, 3 * Q, D // 2, n // 2
    CP = up_to(C3, 128)
    MQ = up_to(-(-MODW // BLKS), 256)
    WE, WL = up_to(5 * D, 1024), up_to(2 * D + 4 * up_to(Q, 128), 1024)
    vm = pl.BlockSpec(memory_space=pltpu.VMEM)
    hbm = pl.BlockSpec(memory_space=pl.ANY)
    out_shape = (
        jax.ShapeDtypeStruct((T, D), BF),
        jax.ShapeDtypeStruct((T, D), BF),
        jax.ShapeDtypeStruct((n, 8, R), F32),
        jax.ShapeDtypeStruct((n, 8, R), F32),
        jax.ShapeDtypeStruct((BLKS, n, 16, WE // 8), BF),
        jax.ShapeDtypeStruct((BLKS, n, 16, WL // 8), BF),
        jax.ShapeDtypeStruct((BLKS, Fr, D), BF),
        jax.ShapeDtypeStruct((BLKS, R, F), BF),
        jax.ShapeDtypeStruct((BLKS, R, CP), BF),
        jax.ShapeDtypeStruct((R, D), BF),
        jax.ShapeDtypeStruct((L, D), BF),
    )
    dma = pltpu.SemaphoreType.DMA
    scratch = [
        pltpu.VMEM((D, C3), BF),
        pltpu.VMEM((2, D, WH), BF),
        pltpu.VMEM((D, F), BF),
        pltpu.VMEM((F, D), BF),
        pltpu.VMEM((R, MQ), BF),
        pltpu.VMEM((1, C3), F32),
        pltpu.VMEM((1, F), F32),
        pltpu.VMEM((1, MODW), F32),
        pltpu.VMEM((n, 8, R), F32),
        pltpu.VMEM((n, 16, MQ // 2), BF),
        pltpu.VMEM((n, 16, MQ // 2), BF),
        pltpu.VMEM((BLKS, 8, MQ), F32),
        pltpu.VMEM((24, MODW), BF),
        pltpu.VMEM((L, D), BF),
        pltpu.VMEM((L, D), BF),
        pltpu.VMEM((L, F), BF),
        pltpu.VMEM((L, F), BF),
        pltpu.VMEM((3 * hpd, L, HD), BF),
        pltpu.VMEM((L, hpd + 1), F32),
        pltpu.VMEM((BLKS, T, Q), BF),
        pltpu.VMEM((BLKS, T, Q), BF),
        pltpu.VMEM((BLKS, T, Q), BF),
        pltpu.VMEM((T, D), F32),
        pltpu.VMEM((T, D), F32),
        pltpu.VMEM((T, D), F32),
        pltpu.VMEM((L, D), BF),
        pltpu.VMEM((3, T, D), BF),
        pltpu.VMEM((3, T, D), BF),
        pltpu.VMEM((F, D), BF),
        pltpu.VMEM((D, F), BF),
        pltpu.VMEM((Q, D), BF),
        pltpu.VMEM((2, nz, R, D), BF),
        pltpu.VMEM((2, nz, R, F), BF),
        pltpu.VMEM((2, nz, R, CP), BF),
        pltpu.VMEM((R, D), BF),
        pltpu.VMEM((nz - 1, R, D), BF),
        pltpu.VMEM((R, D), BF),
        pltpu.VMEM((L, HD), F32),
        pltpu.VMEM((L, HD), F32),
        pltpu.VMEM((8, WE), F32),
        pltpu.VMEM((8, WL), F32),
        pltpu.VMEM((BLKS, 16, WE // 8), BF),
        pltpu.VMEM((BLKS, 16, WL // 8), BF),
        pltpu.VMEM((BLKS, 16, WE // 8), BF),
        pltpu.VMEM((BLKS, 16, WL // 8), BF),
        pltpu.VMEM((n, 8, R), F32),
        dma((18,)),
        dma((4, 4, nz)), dma((4, 4, nz)), dma((1,)), dma((1,)),
        dma((n,)), dma((n,)), dma((n,)), dma((n,)),
        dma((4,)), dma((4,)),
        dma((4, 3)), dma((4, 3)),
        dma((2, 4)), dma((2, 4)),
        dma((3, 3)), dma((3, 3)),
        dma((3, 4, nz)), dma((3, 4, nz)),
        dma((3, 3)), dma((3, 3)),
        dma((2, 4)), dma((2, 4)), dma((2, n)), dma((2, n)), dma((2, 4)), dma((2, 4)),
        dma((n,)), dma((n,)),
        dma((nz + 2,)), dma((nz + 2,)),
    ]
    in_specs = [vm] * 10 + [hbm] * 5
    out_specs = [vm] * 6 + [hbm] * 5
    return pl.pallas_call(
        functools.partial(layer_kernel, dims),
        out_shape=out_shape,
        in_specs=in_specs,
        out_specs=out_specs,
        scratch_shapes=scratch,
        compiler_params=pltpu.CompilerParams(
            collective_id=0, has_side_effects=True, vmem_limit_bytes=63 << 20
        ),
        name="layer",
    )(*inputs)


def finish_kernel(dims, *refs):
    T, D, n, sub, R, Q, HD, hpd, F, Fr, MODW = dims
    CP, QP = up_to(3 * Q, 128), up_to(Q, 128)
    WE, WL = up_to(5 * D, 1024), up_to(2 * D + 4 * QP, 1024)
    HE, HL = WE // 8, WL // 8
    (
        cond_in, cond_rx, dcond, ball_e, ball_l, gd, gu, gq, gw, out_h, gtok_h,
        gcond_o, gqb_o, gvb_o, gob_o, gub_o, gdb_o, gab_o, ga_h, gq_h, gw_h, gu_h, gd_h, out_to, gtok_to,
        stage, sem, *staged,
    ) = refs
    sources = (cond_rx, dcond, ball_e, ball_l, gd, gu, gq, gw, out_h, gtok_h)
    loads = [pltpu.make_async_copy(src, to, sem.at[stage.shape[0] + 2 + i]) for i, (src, to) in enumerate(zip(sources, staged))]
    for copy in loads:
        copy.start()
    cond_rx, dcond, ball_e, ball_l, gd, gu, gq, gw, out_h, gtok_h = staged
    crops = cond_in.shape[0]
    moves = [
        pltpu.make_async_copy(out_h, out_to, sem.at[stage.shape[0]]),
        pltpu.make_async_copy(gtok_h, gtok_to, sem.at[stage.shape[0] + 1]),
    ]

    def put(value, dest):
        slot = len(moves) - 2
        stage[slot] = value
        copy = pltpu.make_async_copy(stage.at[slot], dest, sem.at[slot])
        copy.start()
        moves.append(copy)

    def columns(dest, p):
        return dest.at[:, pl.ds(D * p, D)]

    for copy in loads:
        copy.wait()
    for copy in moves:
        copy.start()
    for j in range(BLKS):
        put(gd[j].astype(F32), gd_h.at[pl.ds(Fr * j, Fr), :])
    for p in range(3):
        put(jnp.concatenate([gq[j, :, Q * p : Q * (p + 1)] for j in range(BLKS)], axis=1).astype(F32), columns(gq_h, p))
    put(gw[...].astype(F32), gw_h)
    for p in range(BLKS):
        width = n // BLKS
        own = [gu[j, :, Fr * i : Fr * (i + 1)] for i in range(width * p, width * (p + 1)) for j in range(BLKS)]
        put(jnp.concatenate(own, axis=1).astype(F32), columns(gu_h, p))

    cond_all = cond_rx[...].reshape(n * 8, R).astype(BF)

    def crop_rows(ball, chunk, half):
        part = ball[chunk // 2].astype(F32)
        return part[:, 0:8, :] if chunk % 2 == 0 else part[:, 8:16, :]

    chunks_e = [crop_rows(ball_e, c, HE) for c in range(8)]
    chunks_l = [crop_rows(ball_l, c, HL) for c in range(8)]

    def slices(size, first, width):
        at = first
        while at < first + width:
            chunk = at // size
            end = min(first + width, size * (chunk + 1))
            yield chunk, at - size * chunk, end - size * chunk
            at = end

    def crop_sums(chunks, size, first, width):
        got = [jnp.sum(chunks[c][:, :, lo:hi], axis=0) for c, lo, hi in slices(size, first, width)]
        return jnp.concatenate(got, axis=1)

    def crop_grads(chunks, size, first):
        got = [tn(cond_all, chunks[c][:, :, lo:hi].reshape(n * 8, hi - lo).astype(BF)) for c, lo, hi in slices(size, first, D)]
        return jnp.concatenate(got, axis=1)

    every = []
    for p in range(6):
        chunks, size, first = (chunks_l, HL, D * p) if p < 2 else (chunks_e, HE, D * (p - 2))
        put(crop_grads(chunks, size, first), columns(ga_h, p))
        sums = crop_sums(chunks, size, first, D)
        every.append(jnp.sum(sums[:crops], axis=0, keepdims=True))
    biases = crop_sums(chunks_e, HE, 4 * D, D)
    gab_o[...] = jnp.concatenate(every, axis=1).reshape(-1)
    gob_o[...] = biases[0]
    gdb_o[...] = biases[1]
    up_sums = crop_sums(chunks_e, HE, 0, BLKS * F)[7:8]
    own = [up_sums[:, F * j + Fr * i : F * j + Fr * (i + 1)] for i in range(n) for j in range(BLKS)]
    gub_o[...] = jnp.concatenate(own, axis=1).reshape(-1)
    biases = crop_sums(chunks_l, HL, 2 * D, BLKS * QP)
    for row, dest in ((0, gqb_o), (1, gvb_o)):
        own = [biases[row : row + 1, QP * j : QP * j + Q] for j in range(BLKS)]
        dest[...] = jnp.concatenate(own, axis=1).reshape(-1)
    grad = jnp.concatenate([dcond[i] for i in range(n)], axis=1)[:crops]
    cond = cond_in[...].astype(F32)
    gate = 1.0 / (1.0 + jnp.exp(-cond))
    gcond_o[...] = grad * (gate + cond * gate * (1.0 - gate))
    for copy in moves:
        copy.wait()


def run_finish(dims, inputs):
    T, D, n, sub, R, Q, HD, hpd, F, Fr, MODW = dims
    crops = inputs[0].shape[0]
    vm = pl.BlockSpec(memory_space=pltpu.VMEM)
    hbm = pl.BlockSpec(memory_space=pl.ANY)
    small = [(crops, D)] + [(width,) for width in (D, D, D, BLKS * F, D, MODW)]
    large = [(R, MODW), (R, 3 * D), (R, D), (R, BLKS * F), (BLKS * Fr, D)]
    pieces = 4 + 3 + 1 + 4 + 6
    return pl.pallas_call(
        functools.partial(finish_kernel, dims),
        out_shape=[jax.ShapeDtypeStruct(shape, F32) for shape in small + large]
        + [jax.ShapeDtypeStruct((T, D), BF)] * 2,
        in_specs=[vm] + [hbm] * (len(inputs) - 1),
        out_specs=[vm] * len(small) + [hbm] * (len(large) + 2),
        scratch_shapes=[pltpu.VMEM((pieces, R, D), F32), pltpu.SemaphoreType.DMA((pieces + 12,))]
        + [pltpu.VMEM(a.shape, a.dtype) for a in inputs[1:]],
        compiler_params=pltpu.CompilerParams(vmem_limit_bytes=62 << 20),
        name="finish",
    )(*inputs)


def per_device(sub, tokens, condition, segment_ids, qkv_weight, query_bias, value_bias, output_weight, output_bias,
               up_weight, up_bias, down_weight, down_bias, adaln_weight, adaln_bias, cotangent):
    T, D = tokens.shape[1:]
    blks, size = lax.axis_size("blk"), lax.axis_size("dp")
    assert blks == BLKS and tokens.shape[0] == 1
    n = size // sub
    HD = D // HEADS
    hpd = HEADS // blks
    Q = D // blks
    FF = up_weight.shape[1]
    MODW = adaln_weight.shape[1]
    F = FF // blks
    R, Fr = D // n, F // n
    dp = lax.axis_index("dp")
    assert FF == 4 * D and MODW == 6 * D and n % BLKS == 0

    def members(step):
        return [(i, i - i % sub + (i + step) % sub) for i in range(size)]

    def collect(w):
        if sub == 1:
            return w
        full = jnp.zeros((sub,) + w.shape, w.dtype)
        for step in range(sub):
            moved = lax.ppermute(w, "dp", members(step)) if step else w
            full = lax.dynamic_update_index_in_dim(full, moved, (dp - step) % sub, 0)
        return full.reshape((-1,) + w.shape[1:])

    def settle(grad):
        if sub == 1:
            return grad
        parts = grad.reshape((sub, -1) + grad.shape[1:])
        total = 0.0
        for step in range(sub):
            part = lax.dynamic_index_in_dim(parts, (dp + step) % sub, 0, keepdims=False)
            total = total + (lax.ppermute(part, "dp", members(step)) if step else part)
        return total

    def over_members(vector):
        if sub == 1:
            return vector
        total = vector
        for step in range(1, sub):
            total = total + lax.ppermute(vector, "dp", members(step))
        return total

    inputs = (
        tokens[0], cotangent[0], segment_ids, condition[0], query_bias, value_bias, output_bias, down_bias,
        up_bias, adaln_bias, collect(adaln_weight), collect(qkv_weight),
        collect(output_weight), collect(up_weight), collect(down_weight),
    )
    dims = (T, D, n, sub, R, Q, HD, hpd, F, Fr, MODW)
    out, gtok, cond_rx, dcond, ball_e, ball_l, gd, gu, gq, gw, _ = run_layer(dims, inputs)
    done = run_finish(dims, (condition[0], cond_rx, dcond, ball_e, ball_l, gd, gu, gq, gw, out, gtok))
    gcond, gqb, gvb, gob, gub, gdb, gab, ga, gq, gw, gu, gd, out, gtok = done
    gqb, gvb, gob, gub, gdb, gab = (over_members(v) for v in (gqb, gvb, gob, gub, gdb, gab))
    ga, gq, gw, gu, gd = (settle(v) for v in (ga, gq, gw, gu, gd))
    return out[None], gtok[None], gcond[None], gq, gqb, gvb, gw, gob, gu, gub, gd, gdb, ga, gab


def solution(mesh):
    rows, strips = P("dp", None), P("dp", "blk", None)
    in_specs = (
        strips, P("dp", None, None), rows, rows, P(), P(), rows, P(), rows, P(), rows, P(), rows, P(), strips,
    )
    out_specs = (
        strips, strips, P("dp", None, None), rows, P(), P(), rows, P(), rows, P(), rows, P(), rows, P(),
    )

    def whole(*args):
        size = mesh.shape["dp"]
        rows_each = args[3].shape[0] // size
        sub = 1
        while (rows_each * sub) % 16:
            sub *= 2
        body = functools.partial(per_device, sub)
        return jax.shard_map(body, mesh=mesh, in_specs=in_specs, out_specs=out_specs, check_vma=False)(*args)

    return whole
```

```python
import functools
import math

import jax
import jax.numpy as jnp
from jax import lax
from jax.experimental import pallas as pl
from jax.experimental.pallas import tpu as pltpu
from jax.sharding import PartitionSpec as P

HEADS = 16
BLKS = 4
BF = jnp.bfloat16
F32 = jnp.float32
MESH = pl.DeviceIdType.MESH
EPS = 1e-06


def up_to(value, multiple):
    return -(-value // multiple) * multiple


def nn(a, b):
    return lax.dot_general(a, b, (((1,), (0,)), ((), ())), preferred_element_type=F32)


def nt(a, b):
    return lax.dot_general(a, b, (((1,), (1,)), ((), ())), preferred_element_type=F32)


def tn(a, b):
    return lax.dot_general(a, b, (((0,), (0,)), ((), ())), preferred_element_type=F32)


def row_sums(values):
    return nn(jnp.ones((8, values.shape[0]), BF), values)[0:1]


def unit_rows(rows):
    centre = rows - jnp.mean(rows, axis=-1, keepdims=True)
    inverse = lax.rsqrt(jnp.mean(centre * centre, axis=-1, keepdims=True) + EPS)
    return centre * inverse, inverse


def norm_back(grad, normed, inverse):
    mean_grad = jnp.mean(grad, axis=-1, keepdims=True)
    mean_both = jnp.mean(grad * normed, axis=-1, keepdims=True)
    return inverse * (grad - mean_grad - normed * mean_both)


def layer_kernel(dims, *refs):
    T, D, n, sub, R, Q, HD, hpd, F, Fr, MODW = dims
    L, C3, WH, nz = BLKS * T, 3 * Q, D // 2, n // 2
    CP, WP = up_to(C3, 128), up_to(WH, 128)
    MQ = up_to(-(-MODW // BLKS), 256)
    WE, WL = up_to(5 * D, 1024), up_to(2 * D + 4 * up_to(Q, 128), 1024)
    QE, QL = WE // 4, WL // 4
    QP = up_to(Q, 128)
    factor = HD ** (-0.5)
    (
        lab_row, cond_in, query_b, value_b, out_bias, down_bias, up_bias, ad_bias,
        x_h, cot_h, ad_h, wq_h, wo_h, wu_h, wd_h,
        out_o, gtok_o, cond_rx, dcond_o, ball_e, ball_l, gd_o, gu_o, gq_o, gw_o, na_h,
        x_in, cot_in, attf, wq, wo, wu, wd, ad, qkv_b, up_b, ad_b, cond_tx, pm_tx, pm_rx, mod4, mod3,
        na, dbm, act, gp, q3, lse, att_tx, att_rx, datt_tx, mid, dmid, bra,
        ps, rs_a, rs_b, gd, gu, pair_w, gd_x, gu_x, gq_x, gw_x, gw_y, dk_acc, dv_acc, sb_e, sb_l, btx_e, btx_l, brx_e, brx_l, dc_tx,
        loc, g_s, g_r, o_s, o_r, c_s, c_r, p_s, p_r, m_s, m_r, ag_s, ag_r, a_s, a_r, r_s, r_r,
        x_s, x_r, f_s, f_r, b1_s, b1_r, b2_s, b2_r, b3_s, b3_r, d_s, d_r, w_s, w_r,
    ) = refs

    dp = lax.axis_index("dp")
    b = lax.axis_index("blk")
    g, member = dp // sub, dp % sub
    zi, xi = g // 2, g % 2
    core = b % 2
    b1, b2, b3 = b + 1 - 2 * core, (b + 2) % 4, 3 - b

    def rel(k):
        return ((b // 2 + k // 2) % 2) * 2 + (b % 2 + k % 2) % 2

    def at_dp(group):
        return (group * sub + member, b)

    def at_blk(index):
        return (dp, index)

    gx = g + 1 - 2 * xi

    place = zi + xi * (n - 1 - 2 * zi)
    first_rows = up_to(R // 2, 16)

    def group_at(position):
        position = (position + 2 * n) % n
        back = position // nz
        return 2 * (position + back * (n - 1 - 2 * position)) + back

    def remote(src, dst, ssem, rsem, where):
        return pltpu.make_async_remote_copy(
            src_ref=src, dst_ref=dst, send_sem=ssem, recv_sem=rsem, device_id=where, device_id_type=MESH
        )

    def strip(i):
        return pl.ds(pl.multiple_of(T * i, T), T)

    def rows_of(i, size):
        return pl.ds(pl.multiple_of(size * i, size), size)

    FF = BLKS * F
    stage_cp = [
        pltpu.make_async_copy(src.at[:, pl.ds(D * p, D)], gd.at[pl.ds(R * to, R), :], loc.at[10 + to])
        for to, (src, p) in enumerate(
            [(wq_h, 0), (wq_h, 1), (wq_h, 2), (wo_h, 0), (wu_h, 0), (wu_h, 1), (wu_h, 2), (wu_h, 3)]
        )
    ]
    for cp in stage_cp:
        cp.start()
    own_d = pltpu.make_async_copy(wd_h.at[rows_of(b, Fr), :], wd.at[rows_of(g, Fr), :], loc.at[3])
    own_d.start()
    x_cp = pltpu.make_async_copy(x_h, x_in, loc.at[0])
    cot_cp = pltpu.make_async_copy(cot_h, cot_in, loc.at[1])
    back_cp = pltpu.make_async_copy(cot_h, dbm.at[strip(b), :], loc.at[2])
    back_cp.start()
    x_cp.start()
    cot_cp.start()

    def flat(ref):
        return ref[...].astype(F32).reshape(1, -1)

    ad_b[...] = flat(ad_bias)

    barrier = pltpu.get_barrier_semaphore()
    for k in range(1, n):
        pl.semaphore_signal(barrier, inc=1, device_id=at_dp((g + k) % n), device_id_type=MESH)
    for other in (b1, b2, b3):
        pl.semaphore_signal(barrier, inc=1, device_id=at_blk(other), device_id_type=MESH)
    pl.semaphore_wait(barrier, n - 1 + 3)

    cond = cond_in[...].astype(F32)
    cond = (cond / (1.0 + jnp.exp(-cond))).astype(BF).astype(F32)
    cond = jnp.concatenate([cond, jnp.zeros((8 - cond.shape[0], D), F32)], axis=0)
    for gg in range(n):
        cond_tx[gg] = cond[:, R * gg : R * (gg + 1)]
    cond_rx[g] = cond_tx[g]
    cond_cp = [
        remote(cond_tx.at[(g + k) % n], cond_rx.at[g], c_s.at[k], c_r.at[k], at_dp((g + k) % n))
        for k in range(1, n)
    ]
    for cp in cond_cp:
        cp.start()

    def piece(size, i, half):
        first = first_rows if half else 0
        return pl.ds(pl.multiple_of(size * i + first, 16), size - first_rows if half else first_rows)

    class Gather:
        def __init__(self, slot, ref):
            self.copies = {}
            for way in range(2):
                sign = 1 - 2 * way
                for half in range(2):
                    for step in range(nz if half == way else nz - 1):
                        at = ref.at[piece(R, group_at(place - sign * step), half), :]
                        flow = 2 * way + half
                        self.copies[way, half, step] = remote(
                            at, at, g_s.at[slot, flow, step], g_r.at[slot, flow, step], at_dp(group_at(place + sign))
                        )

        def start(self, halves=(0, 1)):
            for half in halves:
                for way in range(2):
                    self.copies[way, half, 0].start()

        def hop(self, step):
            for half in range(2):
                for way in range(2):
                    self.copies[way, half, step - 1].wait_recv()
                    if (way, half, step) in self.copies:
                        self.copies[way, half, step].start()

        def arrive(self):
            for way in range(2):
                self.copies[way, way, nz - 1].wait_recv()

        def done(self):
            for copy in self.copies.values():
                copy.wait_send()

    class Spread:
        def __init__(self, slot, buffer, first=0, size=T):
            def copy(index, src, where):
                at = buffer.at[pl.ds(pl.multiple_of(T * src + first, 16), size), :]
                return remote(at, at, ag_s.at[slot, index], ag_r.at[slot, index], at_blk(where))

            self.near, self.far, self.onward = copy(0, b, b1), copy(1, b, b2), copy(2, b2, b1)

        def start(self):
            self.far.start()
            self.near.start()

        def forward(self):
            self.far.wait_recv()
            self.onward.start()

        def arrive(self):
            self.near.wait_recv()
            self.onward.wait_recv()

        def done(self):
            self.near.wait_send()
            self.far.wait_send()
            self.onward.wait_send()

    take_q, take_o = Gather(0, wq), Gather(1, wo.at[core])
    take_u, take_d = Gather(2, wu), Gather(3, wd)
    for cp in stage_cp[:3]:
        cp.wait()
    for j in range(BLKS):

        @pl.when(b == j)
        def _():
            own = [gd[R * p : R * (p + 1), Q * j : Q * (j + 1)] for p in range(3)]
            wq[rows_of(g, R), :] = jnp.concatenate(own, axis=1)

    take_q.start((0,))
    back_cp.wait()
    spread_d = [Spread(1, dbm, 0, T // 2), Spread(4, dbm, T // 2, T // 2)]
    spread_d[0].start()
    start = pl.multiple_of(jnp.minimum(MQ * b, MODW - MQ), 128)
    ad_cp = pltpu.make_async_copy(ad_h.at[:, pl.ds(start, MQ)], ad, loc.at[4])
    ad_cp.start()

    for cp in cond_cp:
        cp.wait_recv()
    ad_cp.wait()
    cond_all = cond_rx[...].reshape(n * 8, R).astype(BF)
    partial = nn(cond_all, ad[...]).reshape(n, 8, MQ)
    halves = jnp.concatenate([partial[:, :, : MQ // 2], partial[:, :, MQ // 2 :]], axis=1)
    pm_tx[...] = halves.astype(BF)
    pm_rx[g] = pm_tx[g]
    part_cp = [
        remote(pm_tx.at[(g + k) % n], pm_rx.at[g], p_s.at[k], p_r.at[k], at_dp((g + k) % n))
        for k in range(1, n)
    ]
    for cp in part_cp:
        cp.start()
    take_q.start((1,))
    for cp in stage_cp[3:]:
        cp.wait()
    for j in range(BLKS):

        @pl.when(b == j)
        def _():
            own = [
                gd[R * (4 + (p // D)) : R * (5 + (p // D)), p % D : p % D + Fr]
                for p in range(Fr * j, FF, BLKS * Fr)
            ]
            wu[rows_of(g, R), :] = jnp.concatenate(own, axis=1)
            at = slice(Q * j, Q * (j + 1))
            parts = [flat(query_b)[:, at], jnp.zeros((1, Q), F32), flat(value_b)[:, at]]
            qkv_b[...] = jnp.concatenate(parts, axis=1)
            every = flat(up_bias)
            own = [every[:, p : p + Fr] for p in range(Fr * j, FF, BLKS * Fr)]
            up_b[...] = jnp.concatenate(own, axis=1)

    for j in range(2):

        @pl.when(core == j)
        def _():
            wo[j, rows_of(g, R), :] = gd[3 * R : 4 * R, WH * j : WH * (j + 1)]

    one_hot = lab_row[...] == lax.broadcasted_iota(jnp.int32, (8, L), 0)
    column = lax.broadcasted_iota(jnp.int32, (8, 128), 0).astype(BF)
    labels = tn(one_hot.astype(BF), column)
    lse[:, hpd : hpd + 1] = labels[:, 0:1]
    row_labels = lab_row[...].astype(F32)
    x_cp.wait()
    for cp in part_cp:
        cp.wait_recv()
    total = jnp.sum(pm_rx[...].astype(F32), axis=0)
    own_mod = jnp.concatenate([total[:8], total[8:]], axis=1) + ad_b[:, pl.ds(start, MQ)]
    mod4[b] = own_mod
    mod_cp = [
        remote(mod4.at[b], mod4.at[b], m_s.at[k], m_r.at[k], at_blk(rel(k))) for k in range(1, 4)
    ]
    for cp in mod_cp:
        cp.start()
    take_q.hop(1)
    for cp in mod_cp:
        cp.wait_recv()
    for j in range(BLKS):
        first = min(MQ * j, MODW - MQ)
        skip = MQ * j - first
        value = mod4[j][:, skip:]
        high = value.astype(BF).astype(F32)
        middle = (value - high).astype(BF).astype(F32)
        parts = jnp.concatenate([high, middle, value - high - middle], axis=0)
        mod3[:, MQ * j : min(MQ * (j + 1), MODW)] = parts.astype(BF)
    CH = T // 2

    def by_chunk(step):
        def body(c, carry):
            step(pl.ds(pl.multiple_of(CH * c, CH), CH), pl.ds(pl.multiple_of(T * b + CH * c, CH), CH))
            return carry

        lax.fori_loop(0, T // CH, body, 0)

    def crop_of(rows, width):
        crops = jnp.bitwise_and(lax.broadcasted_iota(jnp.int32, (CH, width), 1), 7).astype(F32)
        return (lse[rows, hpd : hpd + 1] == crops).astype(BF)

    def per_token(chooser, piece):
        return nn(chooser, mod3[:, D * piece : D * (piece + 1)])

    def per_crop(chooser, values):
        high = values.astype(BF)
        return tn(chooser, high) + tn(chooser, (values - high.astype(F32)).astype(BF))

    def begin(at, rows):
        normed, _ = unit_rows(x_in[at, :].astype(F32))
        chooser = crop_of(rows, 24)
        na[rows, :] = (normed * (1.0 + per_token(chooser, 1)) + per_token(chooser, 0)).astype(BF)

    by_chunk(begin)
    spread_a = Spread(0, na)
    spread_a.start()

    spread_d[1].start()
    sb_e[...] = jnp.zeros_like(sb_e)
    sb_l[...] = jnp.zeros_like(sb_l)
    take_q.hop(2)
    spread_d[0].forward()
    take_q.hop(3)
    take_o.start()
    take_q.arrive()

    def project(k):
        i = rel(k)
        packed = nn(na[strip(i), :], wq[...]) + qkv_b[...]
        for s in range(3 * hpd):
            q3[s, strip(i), :] = packed[:, HD * s : HD * (s + 1)].astype(BF)

    def project_loop(lo, hi):
        def body(k, carry):
            project(k)
            return carry

        lax.fori_loop(lo, hi, body, 0)

    project_loop(0, 1)
    spread_a.near.wait_recv()
    project_loop(1, 2)
    spread_a.forward()
    project_loop(2, 3)
    take_o.hop(1)
    spread_a.onward.wait_recv()
    project_loop(3, 4)
    keep_na = pltpu.make_async_copy(na, na_h, loc.at[5])
    keep_na.start()
    own_d.wait()

    def attend(i):
        mask = lse[strip(i), hpd : hpd + 1] == row_labels
        pieces, logs = [], []
        for h in range(hpd):
            scores = nt(q3[h, strip(i), :], q3[hpd + h]) * factor
            scores = jnp.where(mask, scores, -1e30)
            top = jnp.max(scores, axis=-1, keepdims=True)
            raised = jnp.exp(scores - top)
            sums = jnp.sum(raised, axis=-1, keepdims=True)
            pieces.append(nn(raised.astype(BF), q3[2 * hpd + h]) / sums)
            logs.append(top + jnp.log(sums))
        att_tx[i] = jnp.concatenate(pieces, axis=1).astype(BF)
        lse[strip(i), 0:hpd] = jnp.concatenate(logs, axis=1)

    att_cp = {
        k: remote(att_tx.at[rel(k)], att_rx.at[b], a_s.at[0, k], a_r.at[0, k], at_blk(rel(k)))
        for k in range(1, 4)
    }
    for turn, k in enumerate((2, 3, 1, 0)):
        attend(rel(k))
        if turn == 0:
            keep_na.wait()
            spread_a.done()
        if k:
            att_cp[k].start()
        if turn == 0:
            take_o.hop(2)
        if turn == 1:
            take_o.hop(3)
            take_u.start()
            spread_d[1].forward()
        if turn == 2:
            take_o.arrive()
            share_o = remote(wo.at[core], wo.at[core], o_s.at[0], o_r.at[0], at_blk(b1))
            share_o.start()
    att_rx[b] = att_tx[b]
    for part in spread_d:
        part.arrive()
        part.done()

    def gate(c, carry):
        rows = pl.ds(pl.multiple_of(CH * c, CH), CH)
        dbm[rows, :] = (per_token(crop_of(rows, 24), 5) * dbm[rows, :].astype(F32)).astype(BF)
        return carry

    lax.fori_loop(0, L // CH, gate, 0)
    sb_e[1:2, 4 * D : 5 * D] = row_sums(dbm[strip(b), :])
    take_u.hop(1)
    for k in range(1, 4):
        att_cp[k].wait_recv()
    share_o.wait_recv()
    attf[...] = jnp.concatenate([att_rx[j] for j in range(BLKS)], axis=1)
    branch_a = jnp.concatenate([nn(attf[...], wo[0]), nn(attf[...], wo[1])], axis=1) + flat(out_bias)
    bra[...] = branch_a

    def between(at, rows):
        chooser = crop_of(rows, 24)
        middle = x_in[at, :].astype(F32) + per_token(chooser, 2) * bra[at, :]
        mid[at, :] = middle
        normed, _ = unit_rows(middle)
        na[rows, :] = (normed * (1.0 + per_token(chooser, 4)) + per_token(chooser, 3)).astype(BF)

    by_chunk(between)
    spread_m = Spread(2, na)
    spread_m.start()

    c0, c1 = math.sqrt(2.0 / math.pi), 0.044715

    def feed(k):
        i = rel(k)
        hidden = nn(na[strip(i), :], wu[...]) + up_b[...]
        square = hidden * hidden
        bent = jnp.tanh(c0 * (hidden + c1 * hidden * square))
        half = 0.5 * (1.0 + bent)
        act[strip(i), :] = (hidden * half).astype(BF)
        slope = half + 0.5 * hidden * (1.0 - bent * bent) * (c0 * (1.0 + (3.0 * c1) * square))
        gp[strip(i), :] = slope.astype(BF)

    def feed_down(k):
        i = rel(k)
        na[strip(i), :] = nn(act[strip(i), :], wd[...]).astype(BF)

    def loop(lo, hi, step):
        def body(k, carry):
            step(k)
            return carry

        lax.fori_loop(lo, hi, body, 0)

    class Reduce:
        def __init__(self, slot, buffer, rx):
            self.buffer, self.rx = buffer, rx

            def copy(index, src, where):
                return remote(
                    buffer.at[strip(src), :], rx.at[index], r_s.at[slot, index], r_r.at[slot, index], at_blk(where)
                )

            self.near, self.pair = copy(0, b1, b1), copy(1, b3, b1)
            self.far = []
            for half in range(2):
                at = pl.ds(CH * half, CH)
                src = buffer.at[pl.ds(pl.multiple_of(T * b2 + CH * half, CH), CH), :]
                sems = r_s.at[slot, 2 + half], r_r.at[slot, 2 + half]
                self.far.append(remote(src, rx.at[2, at, :], *sems, at_blk(b2)))

        def cross(self):
            self.pair.wait_recv()
            for half in range(2):
                rows = pl.ds(pl.multiple_of(T * b2 + CH * half, CH), CH)
                total = self.buffer[rows, :].astype(F32) + self.rx[1, CH * half : CH * (half + 1), :].astype(F32)
                self.buffer[rows, :] = total.astype(BF)
                self.far[half].start()

        def by_half(self, step):
            self.near.wait_recv()
            for half in range(2):
                self.far[half].wait_recv()
                at = pl.ds(CH * half, CH)
                rows = pl.ds(pl.multiple_of(T * b + CH * half, CH), CH)
                step(at, rows)

        def sent(self):
            for copy in [self.near, self.pair] + self.far:
                copy.wait_send()

        def result(self, at, rows):
            total = self.buffer[rows, :].astype(F32) + self.rx[0, at, :].astype(F32)
            return total + self.rx[2, at, :].astype(F32)

    take_u.hop(2)
    spread_m.near.wait_recv()
    take_u.hop(3)
    take_d.start()
    spread_m.forward()
    spread_m.onward.wait_recv()
    take_u.arrive()
    loop(0, 2, feed)
    take_d.hop(1)
    loop(2, 4, feed)

    def block(way, left):
        return left if way == 0 or left == nz - 1 else nz + left

    class Scatter:
        def __init__(self, slot, grad, rx, dest):
            self.grad, self.rx, self.dest, self.cols = grad, rx, dest, rx.shape[2]
            self.copies = {}
            for way in range(2):
                sign = 1 - 2 * way
                for half in range(2):
                    far = nz if half == way else nz - 1
                    for left in range(far):
                        where = piece(R, 0, half)
                        if left == far - 1:
                            owner = group_at(place + sign * far)
                            src = grad.at[piece(R, owner, half), pl.ds(0, self.cols)]
                        else:
                            src = rx.at[block(way, left + 1), where, :]
                        flow = 2 * way + half
                        self.copies[way, half, left] = remote(
                            src, rx.at[block(way, left), where, :], x_s.at[slot, flow, left], x_r.at[slot, flow, left],
                            at_dp(group_at(place + sign)),
                        )
            if dest is None:
                return
            own = rx.at[0]
            self.local = pltpu.make_async_copy(own, dest.at[b], loc.at[6 + slot])
            self.near = remote(own, dest.at[b], f_s.at[slot, 0], f_r.at[slot, 0], at_blk(b1))
            self.far = remote(own, dest.at[b], f_s.at[slot, 1], f_r.at[slot, 1], at_blk(b2))
            self.onward = remote(dest.at[b2], dest.at[b2], f_s.at[slot, 2], f_r.at[slot, 2], at_blk(b1))

        def start(self):
            for way in range(2):
                self.copies[way, way, nz - 1].start()
            for way in range(2):
                self.copies[way, 1 - way, nz - 2].start()

        def pump(self, left):
            for other in (1, 0):
                for way in range(2):
                    half = 1 - way if other else way
                    if left == nz - 1 and other:
                        continue
                    self.copies[way, half, left].wait_recv()
                    owner = group_at(place + (1 - 2 * way) * left)
                    first = first_rows if half else 0
                    last = R if half else first_rows
                    own = self.grad[piece(R, owner, half), 0 : self.cols].astype(F32)
                    total = own + self.rx[block(way, left), first:last, :].astype(F32)
                    self.rx[block(way, left), first:last, :] = total.astype(BF)
                    self.copies[way, half, left - 1].start()

        def total(self):
            for way in range(2):
                for half in range(2):
                    self.copies[way, half, 0].wait_recv()
            own = self.grad[rows_of(g, R), 0 : self.cols].astype(F32)
            own = own + self.rx[0].astype(F32) + self.rx[block(1, 0)].astype(F32)
            self.rx[0] = own.astype(BF)
            self.far.start()
            self.near.start()
            self.local.start()

        def forward(self):
            self.far.wait_recv()
            self.onward.start()

        def done(self):
            self.near.wait_recv()
            self.onward.wait_recv()
            self.local.wait()
            self.near.wait_send()
            self.far.wait_send()
            self.onward.wait_send()
            for copy in self.copies.values():
                copy.wait_send()

    give_d = Scatter(0, gd, gd_x, gd_o)
    give_u = Scatter(1, gu, gu_x, gu_o)
    give_q = Scatter(2, wu, gq_x, gq_o)

    def hidden_back(k):
        i = rel(k)
        d_active = nt(dbm[strip(i), :], wd[...])
        gp[strip(i), :] = (gp[strip(i), :].astype(F32) * d_active).astype(BF)

    def tiles(size):
        return 384 if size % 384 == 0 else size

    def weight_grad(dest, left, right, size, parts=None):
        step = tiles(size)
        lo, hi = parts or (0, size // step)

        def body(j, carry):
            at = pl.ds(pl.multiple_of(step * j, step), step)
            dest[at, :] = tn(left[:, at], right[...]).astype(BF)
            return carry

        lax.fori_loop(lo, hi, body, 0)

    tiles_d = F // tiles(F)
    weight_grad(gd, act, dbm, F, (0, tiles_d - 1))
    take_d.hop(2)
    weight_grad(gd, act, dbm, F, (tiles_d - 1, tiles_d))
    give_d.start()
    take_d.hop(3)
    take_d.arrive()
    at_e7 = pl.ds(pl.multiple_of(F * b, 128), F)

    def up_back(k):
        i = rel(k)
        ps[strip(i), :] = nt(gp[strip(i), :], wu[...]).astype(BF)

    def back(k):
        hidden_back(k)
        up_back(k)

    reduce_m = Reduce(1, ps, rs_b)
    loop(3, 4, back)
    reduce_m.pair.start()
    loop(2, 3, back)
    reduce_m.cross()
    loop(1, 2, back)
    reduce_m.near.start()
    loop(0, 1, back)
    give_d.pump(3)
    weight_grad(gu, na, gp, D)
    give_u.start()
    up_sums = row_sums(gp[...])
    spread_m.done()
    reduce_f = Reduce(0, na, rs_a)
    loop(3, 4, feed_down)
    reduce_f.pair.start()
    loop(1, 3, feed_down)
    reduce_f.near.start()
    loop(0, 1, feed_down)
    give_d.pump(2)
    na_back = pltpu.make_async_copy(na_h, gp, loc.at[5])
    na_back.start()

    def middle_back(at, rows):
        d_normed = reduce_m.result(at, rows)
        ps[rows, :] = d_normed.astype(BF)
        normed, inverse = unit_rows(mid[at, :])
        chooser = crop_of(rows, 24)
        d_normed = d_normed * (1.0 + per_token(chooser, 4))
        d_middle = cot_in[at, :].astype(F32) + norm_back(d_normed, normed, inverse)
        dmid[at, :] = d_middle
        dbm[rows, :] = (per_token(chooser, 2) * d_middle).astype(BF)

    cot_cp.wait()
    reduce_m.by_half(middle_back)

    own_rows = dbm[strip(b), :]
    d_att = (nt(own_rows[:, :WH], wo[0]) + nt(own_rows[:, WH:], wo[1])).astype(BF)
    for j in range(BLKS):
        datt_tx[j] = d_att[:, Q * j : Q * (j + 1)]
    datt_cp = {
        k: remote(datt_tx.at[rel(k)], att_rx.at[b], a_s.at[1, k], a_r.at[1, k], at_blk(rel(k)))
        for k in range(1, 4)
    }
    for k in (2, 3, 1):
        datt_cp[k].start()
    reduce_f.cross()
    reduce_m.sent()
    give_d.pump(1)
    give_u.pump(3)
    att_rx[b] = datt_tx[b]

    def middle_sums(at, rows):
        chooser = crop_of(rows, 8)
        normed, _ = unit_rows(mid[at, :])
        d_normed = ps[rows, :].astype(F32)
        sb_e[:, 0:D] += per_crop(chooser, dmid[at, :] * bra[at, :])
        sb_e[:, D : 2 * D] += per_crop(chooser, d_normed)
        sb_e[:, 2 * D : 3 * D] += per_crop(chooser, d_normed * normed)

    by_chunk(middle_sums)
    sb_e[0:1, 4 * D : 5 * D] = row_sums(dbm[strip(b), :])
    take_d.done()
    step_w = tiles(D)

    def out_grad(j, carry):
        at = pl.ds(pl.multiple_of(step_w * j, step_w), step_w)
        wd[at, :] = tn(attf[:, at], dbm[strip(b), :]).astype(BF)
        return carry

    lax.fori_loop(0, D // step_w, out_grad, 0)

    def half_columns(which):
        return pl.ds(pl.multiple_of((D - WP) * which, 128), WP)

    pair_cp = remote(wd.at[:, half_columns(1 - core)], pair_w, w_s.at[0], w_r.at[0], at_blk(b1))
    pair_cp.start()

    class Bundle:
        def __init__(self, slot, sums, tx, rx, ball, quarter):
            self.sums, self.tx, self.rx, self.ball, self.quarter = sums, tx, rx, ball, quarter
            self.one = [
                remote(tx.at[rel(k)], rx.at[b], b1_s.at[slot, k], b1_r.at[slot, k], at_blk(rel(k)))
                for k in range(1, 4)
            ]
            self.two = [
                remote(ball.at[b, g], ball.at[b, g], b2_s.at[slot, k], b2_r.at[slot, k], at_dp((g + k) % n))
                for k in range(1, n)
            ]
            def copy(index, src, where):
                return remote(ball.at[src], ball.at[src], b3_s.at[slot, index], b3_r.at[slot, index], at_blk(where))

            self.three = [copy(0, b, b1), copy(1, b, b2), copy(2, b2, b1)]

        def start(self):
            half = self.quarter // 2
            for j in range(BLKS):
                first = self.sums[:, 2 * half * j : 2 * half * j + half]
                second = self.sums[:, 2 * half * j + half : 2 * half * (j + 1)]
                self.tx[j] = jnp.concatenate([first, second], axis=0).astype(BF)
            self.rx[b] = self.tx[b]
            for cp in self.one:
                cp.start()

        def groups(self):
            for cp in self.one:
                cp.wait_recv()
            self.ball[b, g] = jnp.sum(self.rx[...].astype(F32), axis=0).astype(BF)
            for cp in self.two:
                cp.start()

        def share(self):
            for cp in self.two:
                cp.wait_recv()
            for cp in self.three[:2]:
                cp.start()

        def arrive(self):
            self.three[1].wait_recv()
            self.three[2].start()
            self.three[0].wait_recv()
            self.three[2].wait_recv()

        def done(self):
            for cp in self.one + self.two + self.three:
                cp.wait_send()

    bundle_e = Bundle(0, sb_e, btx_e, brx_e, ball_e, QE)
    bundle_l = Bundle(1, sb_l, btx_l, brx_l, ball_l, QL)
    for k in range(1, 4):
        datt_cp[k].wait_recv()

    def head_back(h):
        dk_acc[...] = jnp.zeros_like(dk_acc)
        dv_acc[...] = jnp.zeros_like(dv_acc)

        def body(i, carry):
            at = strip(i)
            query, keys, values = q3[h, at, :], q3[hpd + h], q3[2 * hpd + h]
            mask = lse[at, hpd : hpd + 1] == row_labels
            scores = jnp.where(mask, nt(query, keys) * factor, -1e30)
            probs = jnp.exp(scores - lse[at, h : h + 1])
            d_out = att_rx[i, :, HD * h : HD * (h + 1)]
            kept = att_tx[i, :, HD * h : HD * (h + 1)]
            delta = jnp.sum(d_out.astype(F32) * kept.astype(F32), axis=-1, keepdims=True)
            dv_acc[...] += tn(probs.astype(BF), d_out)
            d_scores = (probs * (nt(d_out, values) - delta)).astype(BF)
            dk_acc[...] += tn(d_scores, query)
            q3[h, at, :] = (nn(d_scores, keys) * factor).astype(BF)
            return carry

        lax.fori_loop(0, BLKS, body, 0)
        q3[hpd + h] = (dk_acc[...] * factor).astype(BF)
        q3[2 * hpd + h] = dv_acc[...].astype(BF)

    class OutScatter(Scatter):
        def __init__(self):
            super().__init__(3, pair_w, gw_x, None)
            half = gw_x.at[0]
            self.across = remote(half, gw_y, w_s.at[1], w_r.at[1], at_blk(b2))
            self.share = remote(gw_y, gw_o.at[core], w_s.at[2], w_r.at[2], at_blk(b1))
            self.keep = pltpu.make_async_copy(gw_y, gw_o.at[core], loc.at[3])

        def join(self):
            pair_cp.wait_recv()

            def body(j, carry):
                rows = rows_of(j, R)
                total = pair_w[rows, :].astype(F32) + wd[rows, half_columns(core)].astype(F32)
                pair_w[rows, :] = total.astype(BF)
                return carry

            lax.fori_loop(0, n, body, 0)
            self.start()

        def total(self):
            for way in range(2):
                for half in range(2):
                    self.copies[way, half, 0].wait_recv()
            own = self.grad[rows_of(g, R), :].astype(F32)
            own = own + self.rx[0].astype(F32) + self.rx[block(1, 0)].astype(F32)
            self.rx[0] = own.astype(BF)
            self.across.start()

        def finish(self):
            self.across.wait_recv()
            total = gw_y[...].astype(F32) + self.rx[0].astype(F32)
            gw_y[...] = total.astype(BF)
            self.share.start()
            self.keep.start()

        def done(self):
            self.share.wait_recv()
            self.keep.wait()
            for copy in [self.across, self.share] + list(self.copies.values()):
                copy.wait_send()

    give_w = OutScatter()
    head_back(0)
    give_d.total()
    give_u.pump(2)
    give_w.join()
    head_back(1)
    pair_cp.wait_send()
    pieces_cp = [
        pltpu.make_async_copy(ad_h.at[:, pl.ds(D * p, D)], wd.at[pl.ds(R * p, R), pl.ds(0, D)], loc.at[10 + p])
        for p in range(6)
    ]
    for cp in pieces_cp:
        cp.start()
    head_back(2)
    give_u.pump(1)
    give_d.forward()
    head_back(3)

    def back_rows(i):
        return jnp.concatenate([q3[s, strip(i), :] for s in range(3 * hpd)], axis=1)

    def qkv_back(k):
        i = rel(k)
        d_packed = back_rows(i)
        act[strip(i), 0:C3] = d_packed
        ps[strip(i), :] = nt(d_packed, wq[...]).astype(BF)

    reduce_a = Reduce(2, ps, rs_b)
    loop(3, 4, qkv_back)
    reduce_a.pair.start()
    loop(2, 3, qkv_back)
    reduce_a.cross()
    loop(1, 2, qkv_back)
    reduce_a.near.start()
    loop(0, 1, qkv_back)
    give_w.pump(3)
    na_back.wait()
    take_u.done()
    step = tiles(D)

    def grad_body(j, carry):
        at = pl.ds(pl.multiple_of(step * j, step), step)
        wu[at, 0:C3] = tn(gp[:, at], act[:, 0:C3]).astype(BF)
        return carry

    lax.fori_loop(0, D // step, grad_body, 0)
    give_q.start()

    def end(at, rows):
        branch_m = reduce_f.result(at, rows) + flat(down_bias)
        out_o[at, :] = (mid[at, :] + per_token(crop_of(rows, 24), 5) * branch_m).astype(BF)
        sb_e[:, 3 * D : 4 * D] += per_crop(crop_of(rows, 8), cot_in[at, :].astype(F32) * branch_m)

    reduce_f.by_half(end)
    reduce_f.sent()
    sb_e[7:8, at_e7] = up_sums
    bundle_e.start()
    give_u.total()
    give_w.pump(2)
    bias_sums = row_sums(act[:, 0:C3])
    pad = jnp.zeros((1, QP - Q), F32)
    at_l = pl.ds(pl.multiple_of(2 * D + QP * b, 128), QP)
    sb_l[0:1, at_l] = jnp.concatenate([bias_sums[:, :Q], pad], axis=1)
    sb_l[1:2, at_l] = jnp.concatenate([bias_sums[:, 2 * Q :], pad], axis=1)

    def token_sums(at, rows):
        chooser = crop_of(rows, 8)
        normed, _ = unit_rows(x_in[at, :].astype(F32))
        d_normed = reduce_a.result(at, rows)
        sb_l[:, 0:D] += per_crop(chooser, d_normed)
        sb_l[:, D : 2 * D] += per_crop(chooser, d_normed * normed)

    reduce_a.by_half(token_sums)
    bundle_l.start()
    bundle_e.groups()
    give_w.pump(1)
    give_q.pump(3)

    def token_back(at, rows):
        normed, inverse = unit_rows(x_in[at, :].astype(F32))
        d_normed = reduce_a.result(at, rows) * (1.0 + per_token(crop_of(rows, 24), 1))
        gtok_o[at, :] = (dmid[at, :] + norm_back(d_normed, normed, inverse)).astype(BF)

    by_chunk(token_back)
    reduce_a.sent()
    bundle_l.groups()
    bundle_e.share()
    give_u.forward()
    give_q.pump(2)
    give_w.total()
    bundle_e.arrive()
    for cp in pieces_cp:
        cp.wait()

    def crop_part(ball, j, columns, half, first, width):
        both = ball[j].astype(F32)
        rows = both[:, 0:8, :] if half == 0 else both[:, 8:16, :]
        rows = rows.reshape(n * 8, columns).astype(BF)
        total, at = 0.0, first
        while at < first + width:
            p = at // D
            end = min(first + width, D * (p + 1))
            total = total + nt(rows[:, at - first : end - first], wd[R * p : R * (p + 1), at - D * p : end - D * p])
            at = end
        return total

    d_cond = jnp.zeros((n * 8, R), F32)
    for j in range(BLKS):
        for half in range(2):
            first = QE * j + half * (QE // 2)
            width = min(QE // 2, 4 * D - first)
            if width > 0:
                d_cond = d_cond + crop_part(ball_e, j, QE // 2, half, 2 * D + first, width)
    bundle_l.share()
    give_q.pump(1)
    give_w.finish()
    bundle_l.arrive()
    for j in range(BLKS):
        for half in range(2):
            first = QL * j + half * (QL // 2)
            width = min(QL // 2, 2 * D - first)
            if width > 0:
                d_cond = d_cond + crop_part(ball_l, j, QL // 2, half, first, width)
    dc_tx[...] = d_cond.reshape(n, 8, R)
    dcond_o[g] = dc_tx[g]
    dcond_cp = [
        remote(dc_tx.at[(g + k) % n], dcond_o.at[g], d_s.at[k], d_r.at[k], at_dp((g + k) % n))
        for k in range(1, n)
    ]
    for cp in dcond_cp:
        cp.start()
    give_q.total()
    give_q.forward()
    for cp in dcond_cp:
        cp.wait_recv()

    give_q.done()
    give_d.done()
    give_u.done()
    give_w.done()
    bundle_e.done()
    bundle_l.done()
    for cp in cond_cp + part_cp + mod_cp + dcond_cp:
        cp.wait_send()
    for k in range(1, 4):
        att_cp[k].wait_send()
        datt_cp[k].wait_send()
    share_o.wait_send()
    for take in (take_q, take_o):
        take.done()


def run_layer(dims, inputs):
    T, D, n, sub, R, Q, HD, hpd, F, Fr, MODW = dims
    L, C3, WH, nz = BLKS * T, 3 * Q, D // 2, n // 2
    CP, WP = up_to(C3, 128), up_to(WH, 128)
    MQ = up_to(-(-MODW // BLKS), 256)
    WE, WL = up_to(5 * D, 1024), up_to(2 * D + 4 * up_to(Q, 128), 1024)
    vm = pl.BlockSpec(memory_space=pltpu.VMEM)
    hbm = pl.BlockSpec(memory_space=pl.ANY)
    out_shape = (
        jax.ShapeDtypeStruct((T, D), BF),
        jax.ShapeDtypeStruct((T, D), BF),
        jax.ShapeDtypeStruct((n, 8, R), F32),
        jax.ShapeDtypeStruct((n, 8, R), F32),
        jax.ShapeDtypeStruct((BLKS, n, 16, WE // 8), BF),
        jax.ShapeDtypeStruct((BLKS, n, 16, WL // 8), BF),
        jax.ShapeDtypeStruct((BLKS, Fr, D), BF),
        jax.ShapeDtypeStruct((BLKS, R, F), BF),
        jax.ShapeDtypeStruct((BLKS, R, CP), BF),
        jax.ShapeDtypeStruct((2, R, WP), BF),
        jax.ShapeDtypeStruct((L, D), BF),
    )
    dma = pltpu.SemaphoreType.DMA
    scratch = [
        pltpu.VMEM((T, D), BF),
        pltpu.VMEM((T, D), BF),
        pltpu.VMEM((T, D), BF),
        pltpu.VMEM((D, C3), BF),
        pltpu.VMEM((2, D, WH), BF),
        pltpu.VMEM((D, F), BF),
        pltpu.VMEM((F, D), BF),
        pltpu.VMEM((R, MQ), BF),
        pltpu.VMEM((1, C3), F32),
        pltpu.VMEM((1, F), F32),
        pltpu.VMEM((1, MODW), F32),
        pltpu.VMEM((n, 8, R), F32),
        pltpu.VMEM((n, 16, MQ // 2), BF),
        pltpu.VMEM((n, 16, MQ // 2), BF),
        pltpu.VMEM((BLKS, 8, MQ), F32),
        pltpu.VMEM((24, MODW), BF),
        pltpu.VMEM((L, D), BF),
        pltpu.VMEM((L, D), BF),
        pltpu.VMEM((L, F), BF),
        pltpu.VMEM((L, F), BF),
        pltpu.VMEM((3 * hpd, L, HD), BF),
        pltpu.VMEM((L, hpd + 1), F32),
        pltpu.VMEM((BLKS, T, Q), BF),
        pltpu.VMEM((BLKS, T, Q), BF),
        pltpu.VMEM((BLKS, T, Q), BF),
        pltpu.VMEM((T, D), F32),
        pltpu.VMEM((T, D), F32),
        pltpu.VMEM((T, D), F32),
        pltpu.VMEM((L, D), BF),
        pltpu.VMEM((3, T, D), BF),
        pltpu.VMEM((3, T, D), BF),
        pltpu.VMEM((F, D), BF),
        pltpu.VMEM((D, F), BF),
        pltpu.VMEM((D, WP), BF),
        pltpu.VMEM((2 * nz - 1, R, D), BF),
        pltpu.VMEM((2 * nz - 1, R, F), BF),
        pltpu.VMEM((2 * nz - 1, R, CP), BF),
        pltpu.VMEM((2 * nz - 1, R, WP), BF),
        pltpu.VMEM((R, WP), BF),
        pltpu.VMEM((L, HD), F32),
        pltpu.VMEM((L, HD), F32),
        pltpu.VMEM((8, WE), F32),
        pltpu.VMEM((8, WL), F32),
        pltpu.VMEM((BLKS, 16, WE // 8), BF),
        pltpu.VMEM((BLKS, 16, WL // 8), BF),
        pltpu.VMEM((BLKS, 16, WE // 8), BF),
        pltpu.VMEM((BLKS, 16, WL // 8), BF),
        pltpu.VMEM((n, 8, R), F32),
        dma((18,)),
        dma((4, 4, nz)), dma((4, 4, nz)), dma((1,)), dma((1,)),
        dma((n,)), dma((n,)), dma((n,)), dma((n,)),
        dma((4,)), dma((4,)),
        dma((5, 3)), dma((5, 3)),
        dma((2, 4)), dma((2, 4)),
        dma((3, 4)), dma((3, 4)),
        dma((4, 4, nz)), dma((4, 4, nz)),
        dma((4, 3)), dma((4, 3)),
        dma((2, 4)), dma((2, 4)), dma((2, n)), dma((2, n)), dma((2, 4)), dma((2, 4)),
        dma((n,)), dma((n,)),
        dma((3,)), dma((3,)),
    ]
    in_specs = [vm] * 8 + [hbm] * 7
    out_specs = [vm] * 6 + [hbm] * 5
    return pl.pallas_call(
        functools.partial(layer_kernel, dims),
        out_shape=out_shape,
        in_specs=in_specs,
        out_specs=out_specs,
        scratch_shapes=scratch,
        compiler_params=pltpu.CompilerParams(
            collective_id=0, has_side_effects=True, vmem_limit_bytes=63 << 20
        ),
        name="layer",
    )(*inputs)


def finish_kernel(dims, *refs):
    T, D, n, sub, R, Q, HD, hpd, F, Fr, MODW = dims
    CP, QP = up_to(3 * Q, 128), up_to(Q, 128)
    WE, WL = up_to(5 * D, 1024), up_to(2 * D + 4 * QP, 1024)
    HE, HL = WE // 8, WL // 8
    (
        cond_in, cond_rx, dcond, ball_e, ball_l, gd, gu, gq, gw, out_h, gtok_h,
        gcond_o, gqb_o, gvb_o, gob_o, gub_o, gdb_o, gab_o, ga_h, gq_h, gw_h, gu_h, gd_h, out_to, gtok_to,
        stage, sem, *staged,
    ) = refs
    sources = (cond_rx, dcond, ball_e, ball_l, gd, gu, gq, gw, out_h, gtok_h)
    loads = [pltpu.make_async_copy(src, to, sem.at[stage.shape[0] + 2 + i]) for i, (src, to) in enumerate(zip(sources, staged))]
    for i in (4, 6, 7, 5, 0, 1, 2, 3, 8, 9):
        loads[i].start()
    cond_rx, dcond, ball_e, ball_l, gd, gu, gq, gw, out_h, gtok_h = staged
    crops = cond_in.shape[0]
    moves = [
        pltpu.make_async_copy(out_h, out_to, sem.at[stage.shape[0]]),
        pltpu.make_async_copy(gtok_h, gtok_to, sem.at[stage.shape[0] + 1]),
    ]

    def put(value, dest):
        slot = len(moves) - 2
        stage[slot] = value
        copy = pltpu.make_async_copy(stage.at[slot], dest, sem.at[slot])
        copy.start()
        moves.append(copy)

    def columns(dest, p):
        return dest.at[:, pl.ds(D * p, D)]

    def ready(*which):
        for i in which:
            loads[i].wait()

    ready(4)
    for j in range(BLKS):
        put(gd[j].astype(F32), gd_h.at[pl.ds(Fr * j, Fr), :])
    ready(6)
    for p in range(3):
        put(jnp.concatenate([gq[j, :, Q * p : Q * (p + 1)] for j in range(BLKS)], axis=1).astype(F32), columns(gq_h, p))
    ready(7)
    WP = gw.shape[2]
    put(jnp.concatenate([gw[0], gw[1, :, 2 * WP - D :]], axis=1).astype(F32), gw_h)
    ready(5)
    for p in range(BLKS):
        width = n // BLKS
        own = [gu[j, :, Fr * i : Fr * (i + 1)] for i in range(width * p, width * (p + 1)) for j in range(BLKS)]
        put(jnp.concatenate(own, axis=1).astype(F32), columns(gu_h, p))

    ready(0, 1, 2, 3, 8, 9)
    for copy in moves[:2]:
        copy.start()
    cond_all = cond_rx[...].reshape(n * 8, R).astype(BF)

    def crop_rows(ball, chunk, half):
        part = ball[chunk // 2].astype(F32)
        return part[:, 0:8, :] if chunk % 2 == 0 else part[:, 8:16, :]

    chunks_e = [crop_rows(ball_e, c, HE) for c in range(8)]
    chunks_l = [crop_rows(ball_l, c, HL) for c in range(8)]

    def slices(size, first, width):
        at = first
        while at < first + width:
            chunk = at // size
            end = min(first + width, size * (chunk + 1))
            yield chunk, at - size * chunk, end - size * chunk
            at = end

    def crop_sums(chunks, size, first, width):
        got = [jnp.sum(chunks[c][:, :, lo:hi], axis=0) for c, lo, hi in slices(size, first, width)]
        return jnp.concatenate(got, axis=1)

    def crop_grads(chunks, size, first):
        got = [tn(cond_all, chunks[c][:, :, lo:hi].reshape(n * 8, hi - lo).astype(BF)) for c, lo, hi in slices(size, first, D)]
        return jnp.concatenate(got, axis=1)

    every = []
    for p in range(6):
        chunks, size, first = (chunks_l, HL, D * p) if p < 2 else (chunks_e, HE, D * (p - 2))
        put(crop_grads(chunks, size, first), columns(ga_h, p))
        sums = crop_sums(chunks, size, first, D)
        every.append(jnp.sum(sums[:crops], axis=0, keepdims=True))
    biases = crop_sums(chunks_e, HE, 4 * D, D)
    gab_o[...] = jnp.concatenate(every, axis=1).reshape(-1)
    gob_o[...] = biases[0]
    gdb_o[...] = biases[1]
    up_sums = crop_sums(chunks_e, HE, 0, BLKS * F)[7:8]
    own = [up_sums[:, F * j + Fr * i : F * j + Fr * (i + 1)] for i in range(n) for j in range(BLKS)]
    gub_o[...] = jnp.concatenate(own, axis=1).reshape(-1)
    biases = crop_sums(chunks_l, HL, 2 * D, BLKS * QP)
    for row, dest in ((0, gqb_o), (1, gvb_o)):
        own = [biases[row : row + 1, QP * j : QP * j + Q] for j in range(BLKS)]
        dest[...] = jnp.concatenate(own, axis=1).reshape(-1)
    grad = jnp.concatenate([dcond[i] for i in range(n)], axis=1)[:crops]
    cond = cond_in[...].astype(F32)
    gate = 1.0 / (1.0 + jnp.exp(-cond))
    grad = grad * (gate + cond * gate * (1.0 - gate))
    for i in range(crops):
        gcond_o[i] = grad[i : i + 1]
    for copy in moves:
        copy.wait()


def run_finish(dims, inputs):
    T, D, n, sub, R, Q, HD, hpd, F, Fr, MODW = dims
    crops = inputs[0].shape[0]
    vm = pl.BlockSpec(memory_space=pltpu.VMEM)
    hbm = pl.BlockSpec(memory_space=pl.ANY)
    small = [(crops, 1, D)] + [(width,) for width in (D, D, D, BLKS * F, D, MODW)]
    large = [(R, MODW), (R, 3 * D), (R, D), (R, BLKS * F), (BLKS * Fr, D)]
    pieces = 4 + 3 + 1 + 4 + 6
    return pl.pallas_call(
        functools.partial(finish_kernel, dims),
        out_shape=[jax.ShapeDtypeStruct(shape, F32) for shape in small + large]
        + [jax.ShapeDtypeStruct((T, D), BF)] * 2,
        in_specs=[vm] + [hbm] * (len(inputs) - 1),
        out_specs=[vm] * len(small) + [hbm] * (len(large) + 2),
        scratch_shapes=[pltpu.VMEM((pieces, R, D), F32), pltpu.SemaphoreType.DMA((pieces + 12,))]
        + [pltpu.VMEM(a.shape, a.dtype) for a in inputs[1:]],
        compiler_params=pltpu.CompilerParams(vmem_limit_bytes=62 << 20),
        name="finish",
    )(*inputs)


def per_device(sub, tokens, condition, segment_ids, qkv_weight, query_bias, value_bias, output_weight, output_bias,
               up_weight, up_bias, down_weight, down_bias, adaln_weight, adaln_bias, cotangent):
    T, D = tokens.shape[1:]
    blks, size = lax.axis_size("blk"), lax.axis_size("dp")
    assert blks == BLKS and tokens.shape[0] == 1
    n = size // sub
    HD = D // HEADS
    hpd = HEADS // blks
    Q = D // blks
    FF = up_weight.shape[1]
    MODW = adaln_weight.shape[1]
    F = FF // blks
    R, Fr = D // n, F // n
    dp = lax.axis_index("dp")
    assert FF == 4 * D and MODW == 6 * D and n % BLKS == 0

    def members(step):
        return [(i, i - i % sub + (i + step) % sub) for i in range(size)]

    def collect(w):
        if sub == 1:
            return w
        full = jnp.zeros((sub,) + w.shape, w.dtype)
        for step in range(sub):
            moved = lax.ppermute(w, "dp", members(step)) if step else w
            full = lax.dynamic_update_index_in_dim(full, moved, (dp - step) % sub, 0)
        return full.reshape((-1,) + w.shape[1:])

    def settle(grad):
        if sub == 1:
            return grad
        parts = grad.reshape((sub, -1) + grad.shape[1:])
        total = 0.0
        for step in range(sub):
            part = lax.dynamic_index_in_dim(parts, (dp + step) % sub, 0, keepdims=False)
            total = total + (lax.ppermute(part, "dp", members(step)) if step else part)
        return total

    def over_members(vector):
        if sub == 1:
            return vector
        total = vector
        for step in range(1, sub):
            total = total + lax.ppermute(vector, "dp", members(step))
        return total

    inputs = (
        segment_ids, condition[0], query_bias, value_bias, output_bias, down_bias, up_bias, adaln_bias,
        tokens[0], cotangent[0], collect(adaln_weight), collect(qkv_weight),
        collect(output_weight), collect(up_weight), collect(down_weight),
    )
    dims = (T, D, n, sub, R, Q, HD, hpd, F, Fr, MODW)
    out, gtok, cond_rx, dcond, ball_e, ball_l, gd, gu, gq, gw, _ = run_layer(dims, inputs)
    done = run_finish(dims, (condition[0], cond_rx, dcond, ball_e, ball_l, gd, gu, gq, gw, out, gtok))
    gcond, gqb, gvb, gob, gub, gdb, gab, ga, gq, gw, gu, gd, out, gtok = done
    gqb, gvb, gob, gub, gdb, gab = (over_members(v) for v in (gqb, gvb, gob, gub, gdb, gab))
    ga, gq, gw, gu, gd = (settle(v) for v in (ga, gq, gw, gu, gd))
    return out[None], gtok[None], gcond.transpose(1, 0, 2), gq, gqb, gvb, gw, gob, gu, gub, gd, gdb, ga, gab


def solution(mesh):
    rows, strips = P("dp", None), P("dp", "blk", None)
    in_specs = (
        strips, P("dp", None, None), rows, rows, P(), P(), rows, P(), rows, P(), rows, P(), rows, P(), strips,
    )
    out_specs = (
        strips, strips, P("dp", None, None), rows, P(), P(), rows, P(), rows, P(), rows, P(), rows, P(),
    )

    def whole(*args):
        size = mesh.shape["dp"]
        rows_each = args[3].shape[0] // size
        sub = 1
        while (rows_each * sub) % 16:
            sub *= 2
        body = functools.partial(per_device, sub)
        return jax.shard_map(body, mesh=mesh, in_specs=in_specs, out_specs=out_specs, check_vma=False)(*args)

    return whole
```
